32 devices in a mesh: dom: 32 (over z, y, x, core).
Axes of the slice: x: 2, y: 2, z: 4, core: 2. Of those that a mesh axis runs over, the one named last changes fastest.
Arguments:
- positions: float32 [1024, 3, 128], P('dom'), may hold values from 0 to 6
- velocities: float32 [1024, 3, 128], P('dom'), may hold values from -6 to 6
- masses: float32 [1024, 128], P('dom'), may hold values from 0.035 to 0.13
- smoothing: float32 [1024, 128], P('dom'), may hold values from 0.8 to 1.4
- entropy: float32 [1024, 128], P('dom'), may hold values from 0.5 to 2
- export_blocks: int32 [32, 32, 32], P('dom'), may hold values from -1 to 31, as said below
- partner_slots: int32 [1024, 16], P('dom'), may hold values from 0 to 1023, as said below
- active: int32 [1024], P('dom'), may hold values from 0 to 1, as said below
Outputs:
- density: float32 [1024, 128], P('dom')
- divergence: float32 [1024, 128], P('dom')
- acceleration: float32 [1024, 3, 128], P('dom')
The draws below stay inside these ranges and needn't reach their ends.
Inputs may be any that keep to these rules, and one draw needn't show every extreme that they name: `export_blocks`: entry [p, d, c] is the index within segment p of the block that p sends to segment d in slot c, or -1 for an empty slot. Filled slots come first; each segment receives 32 filled slots from a quarter of the segments, 16 from half of them and none from the rest. `partner_slots`: for a block of segment d, each entry is p * 32 + c for a filled slot c from segment p to d; every filled slot to d is named exactly once over d's blocks. Every segment has 1 to 32 active blocks, and some segment has all of them active.
All inputs are finite; a program needn't handle non-finite values.
Results may differ from the reference program's by a relative error of at most 0.00002.
Values sent between devices are 32-bit elements; how exact they have to be, the bound alone decides.
No kernel may reach another device: no remote copies, remote signals or barrier semaphores. Data moves between devices by JAX's collectives and lax.ppermute only.
A program may use at most 64 MiB of HBM per device.

```python
import math
import jax
import jax.numpy as jnp
from jax import lax

BLOCK = 128
NB = 32
K_REM = 16
CAP = 32
BLOCKS = 1024
N_DOM = 32


def slot_tables(key):
    quarter = N_DOM // 4
    pattern = jnp.concatenate([jnp.zeros((quarter,), jnp.int32), jnp.full((N_DOM // 2,), CAP // 2, jnp.int32), jnp.full((N_DOM - quarter - N_DOM // 2,), CAP, jnp.int32)])
    count_keys = jax.random.split(jax.random.fold_in(key, 11), N_DOM)
    counts = jax.vmap(lambda single: pattern[jax.random.permutation(single, N_DOM)])(count_keys)
    picks = jax.random.randint(jax.random.fold_in(key, 12), (N_DOM, N_DOM, CAP), 0, NB)
    slot_number = jnp.arange(CAP, dtype=jnp.int32)
    filled = slot_number[None, None, :] < jnp.transpose(counts)[:, :, None]
    exported = jnp.where(filled, picks, -1).astype(jnp.int32)
    filled_recv = jnp.transpose(filled, (1, 0, 2)).reshape(N_DOM, N_DOM * CAP)
    rank_keys = jax.random.split(jax.random.fold_in(key, 13), N_DOM)
    ranking = jax.vmap(lambda single: jax.random.permutation(single, N_DOM * CAP))(rank_keys)
    position = jnp.arange(N_DOM * CAP, dtype=jnp.int32)
    scores = jnp.where(filled_recv, ranking, N_DOM * CAP + position[None, :])
    ordered = jnp.argsort(scores, axis=1, stable=True)[:, :NB * K_REM]
    partner = ordered.reshape(N_DOM * NB, K_REM).astype(jnp.int32)
    return (exported, partner)


def draw_export_blocks(key, part):
    exported, partner = slot_tables(key)
    return exported


def draw_partner_slots(key, part):
    exported, partner = slot_tables(key)
    return partner


def draw_active(key, part):
    device_keys = jax.random.split(jax.random.fold_in(key, 21), N_DOM)

    def single_device(device_key):
        first_key, second_key, third_key = jax.random.split(device_key, 3)
        first_pick = jax.random.randint(first_key, (), 0, NB)
        second_pick = jax.random.randint(second_key, (), 0, NB)
        amount = 1 + first_pick * second_pick // NB
        ranking = jax.random.permutation(third_key, NB)
        return (ranking, amount)
    rankings, amounts = jax.vmap(single_device)(device_keys)
    busiest = jax.random.randint(jax.random.fold_in(key, 22), (), 0, N_DOM)
    amounts = jnp.where(jnp.arange(N_DOM) == busiest, NB, amounts)
    return (rankings < amounts[:, None]).astype(jnp.int32).reshape(N_DOM * NB)


def levels(key, extent, cuts, least, largest):
    factor_of, own = 1.0, jax.random.fold_in(key, 6)
    for dim, shards_of in cuts:
        steps = jnp.exp(jax.random.uniform(jax.random.fold_in(own, dim), (shards_of,), jnp.float32, least / len(cuts), largest / len(cuts)))
        factor_of = factor_of * jnp.repeat(steps, extent[dim] // shards_of).reshape([-1 if axis == dim else 1 for axis in range(len(extent))])
    return factor_of


def gaussian(stream_key, extent, spread, reach, cuts=(), held_as=jnp.bfloat16):
    level = levels(stream_key, extent, cuts, -0.22, 0.18) if cuts else 1.0
    array = jax.random.normal(stream_key, extent, jnp.float32) * spread * level
    return jnp.minimum(jnp.maximum(array, -reach), reach).astype(held_as)


def setup_inputs(seed: int = 0) -> dict:
    streams_of = jax.random.split(jax.random.key(seed), 9)
    positions = jnp.clip(6.0 * jax.random.uniform(streams_of[0], (BLOCKS, 3, BLOCK), jnp.float32) ** levels(streams_of[0], (BLOCKS, 3, BLOCK), ((0, 32),), -0.2, 0.2), 0.0, 6.0)
    velocities = gaussian(streams_of[1], (BLOCKS, 3, BLOCK), 1.0, 6.0, ((0, 32),), jnp.float32)
    masses = jnp.clip(jnp.exp(math.log(0.13) - 1.31218635 * jax.random.uniform(streams_of[2], (BLOCKS, BLOCK), jnp.float32) ** levels(streams_of[2], (BLOCKS, BLOCK), ((0, 32),), -0.2, 0.2)), 0.035, 0.13)
    smoothing = jnp.clip(jnp.exp(math.log(1.4) - 0.55961576 * jax.random.uniform(streams_of[3], (BLOCKS, BLOCK), jnp.float32) ** levels(streams_of[3], (BLOCKS, BLOCK), ((0, 32),), -0.2, 0.2)), 0.8, 1.4)
    entropy = jnp.clip(jnp.exp(math.log(2.0) - 1.3862944 * jax.random.uniform(streams_of[4], (BLOCKS, BLOCK), jnp.float32) ** levels(streams_of[4], (BLOCKS, BLOCK), ((0, 32),), -0.2, 0.2)), 0.5, 2.0)
    export_blocks = draw_export_blocks(jax.random.fold_in(streams_of[8], 71), 0)
    partner_slots = draw_partner_slots(jax.random.fold_in(streams_of[8], 71), 0)
    active = draw_active(jax.random.fold_in(streams_of[8], 71), 0)
    return {"positions": positions, "velocities": velocities, "masses": masses, "smoothing": smoothing, "entropy": entropy, "export_blocks": export_blocks, "partner_slots": partner_slots, "active": active}


kernel_norm = 3.3422538049298023

def kernel_parts(radius, smooth):
    ratio = radius / smooth
    tail = jnp.maximum(1.0 - ratio, 0.0)
    value = kernel_norm * tail ** 4 * (1.0 + 4.0 * ratio) / smooth ** 3
    slope = -20.0 * kernel_norm * tail ** 3 / smooth ** 5
    return (value, slope)

def separation(own_pos, near_pos):
    offset = own_pos[None, :, None, :] - near_pos[:, :, :, None]
    radius = jnp.sqrt(lax.optimization_barrier(jnp.sum(offset * offset, axis=1)))
    return (offset, radius)

def density_block(own_pos, own_vel, own_smooth, near_pos, near_vel, near_mass):
    offset, radius = separation(own_pos, near_pos)
    value, slope = kernel_parts(radius, own_smooth[None, None, :])
    weight = near_mass[:, :, None]
    density = lax.optimization_barrier(jnp.sum(weight * value, axis=(0, 1)))
    moving = own_vel[None, :, None, :] - near_vel[:, :, :, None]
    approach = lax.optimization_barrier(jnp.sum(moving * offset, axis=1))
    divergence = -lax.optimization_barrier(jnp.sum(weight * slope * approach, axis=(0, 1))) / density
    return (density, divergence)

def force_block(own_pos, own_smooth, own_press, near_pos, near_smooth, near_mass, near_press):
    offset, radius = separation(own_pos, near_pos)
    _, slope_own = kernel_parts(radius, own_smooth[None, None, :])
    _, slope_near = kernel_parts(radius, near_smooth[:, :, None])
    factor = near_mass[:, :, None] * (own_press[None, None, :] * slope_own + near_press[:, :, None] * slope_near)
    return -lax.optimization_barrier(jnp.sum(factor[:, None] * offset, axis=(0, 2)))

def reference(positions, velocities, masses, smoothing, entropy, export_blocks, partner_slots, active):
    block_ids = jnp.arange(BLOCKS, dtype=jnp.int32)
    owner = block_ids // NB
    senders = partner_slots // CAP
    within = partner_slots % CAP
    remote = senders * NB + export_blocks[senders, owner[:, None], within]
    local = owner[:, None] * NB + jnp.arange(NB, dtype=jnp.int32)[None, :]
    partners = jnp.concatenate([local, remote], axis=1).astype(jnp.int32)

    def first_pass(member):
        index, chosen = member
        return density_block(positions[index], velocities[index], smoothing[index], positions[chosen], velocities[chosen], masses[chosen])
    density, divergence = lax.map(first_pass, (block_ids, partners))
    pressure_term = entropy * jnp.power(density, -1.0 / 3.0)

    def second_pass(member):
        index, chosen = member
        return force_block(positions[index], smoothing[index], pressure_term[index], positions[chosen], smoothing[chosen], masses[chosen], pressure_term[chosen])
    acceleration = lax.map(second_pass, (block_ids, partners))
    acceleration = jnp.where(active[:, None, None] > 0, acceleration, 0.0)
    return (density, divergence, acceleration)
```

```python
import functools

import jax
import jax.numpy as jnp
import numpy as np
from jax import lax
from jax.experimental import pallas as pl
from jax.experimental.pallas import tpu as pltpu
from jax.sharding import PartitionSpec as P

kernel_norm = 3.3422538049298023
LANES = 128
FEATS = 96
ROWS = 512
CHUNK = 1024
bf16 = jnp.bfloat16
f32 = jnp.float32
NT = (((1,), (1,)), ((), ()))


def split3(value):
    high = value.astype(bf16).astype(f32)
    rest = value - high
    middle = rest.astype(bf16).astype(f32)
    return high, middle, rest - middle


def near_rows(value, extra):
    high, middle, low = split3(value)
    first = [high, middle]
    last = [low, extra]
    return jnp.concatenate(first * 3 + last * 3, axis=0).astype(bf16)


def own_rows(value, extra):
    parts = split3(value)
    rows = []
    for part in parts:
        rows += [part, part]
    for part, more in zip(parts, extra):
        rows += [part, more]
    rows.append(jnp.zeros((LANES - FEATS, LANES), f32))
    return jnp.concatenate(rows, axis=0).T[:, :FEATS].astype(bf16)


def particle_rows(fields, centre):
    shifted = fields - centre
    pos = shifted[0:3]
    vel = shifted[3:6]
    square = jnp.sum(pos * pos, axis=0, keepdims=True)
    cross = jnp.sum(pos * vel, axis=0, keepdims=True)
    return pos, vel, square, cross


def moment_rows(pos, vel, square, cross):
    one = jnp.ones_like(square)
    value = jnp.concatenate([pos, vel, one, cross], axis=0)
    parts = split3(square)
    extra = jnp.concatenate(list(parts) + [jnp.zeros((5, LANES), f32)], axis=0)
    return value, extra


def slope_rows(pos, square, scale, smooth):
    sigma = scale / smooth
    sigma = sigma * sigma
    return jnp.concatenate([pos * sigma, sigma, square * sigma, jnp.zeros((3, LANES), f32)], axis=0)


def prepare_kernel(fields_ref, near_ref, own_ref, own2_ref, mass_ref, centre_ref):
    blocks = fields_ref.shape[0]
    total = jnp.sum(fields_ref[...], axis=0)
    mean = jnp.sum(total, axis=1, keepdims=True) / (blocks * LANES)
    rows = lax.broadcasted_iota(jnp.int32, (8, LANES), 0)
    centre = jnp.where(rows < 6, jnp.broadcast_to(mean, (8, LANES)), 0.0)
    centre_ref[...] = centre
    zero = jnp.zeros((8, LANES), f32)

    @pl.loop(0, blocks)
    def _(index):
        fields = fields_ref[index]
        at = pl.ds(pl.multiple_of(index * LANES, LANES), LANES)
        pos, vel, square, cross = particle_rows(fields, centre)
        value, extra = moment_rows(pos, vel, square, cross)
        near_ref[:, at] = near_rows(value, extra)
        mass_ref[:, at] = fields[6:7]
        smooth = fields[7:8]
        sigma = 16.0 / (smooth * smooth)
        blank = jnp.zeros((3, LANES), f32)
        coefficient = jnp.concatenate(
            [pos * (-2.0 * sigma), blank, square * sigma, blank[0:1]], axis=0
        )
        more = [
            jnp.concatenate([part] * 3 + [jnp.zeros((5, LANES), f32)], axis=0)
            for part in split3(sigma)
        ]
        own_ref[at, :] = own_rows(coefficient, more)
        coefficient = jnp.concatenate(
            [pos * -2.0, square, jnp.ones_like(square), blank], axis=0
        )
        own2_ref[at, :] = own_rows(coefficient, [zero] * 3)


def first_chunk(own, near, mass, moments):
    square = jnp.maximum(jnp.dot(own, near, preferred_element_type=f32), 1e-12)
    tail = jnp.maximum(4.0 - square * lax.rsqrt(square), 0.0)
    fourth = tail * tail
    slope = fourth * tail * mass
    value = slope * (tail * (5.0 - tail))
    width = value.shape[1]
    lanes = value[:, 0:LANES]
    for part in range(LANES, width, LANES):
        lanes = lanes + value[:, part : part + LANES]
    return lanes, reduce_slope(slope, moments)


def second_chunk(own, near, scale, moments):
    square = jnp.maximum(jnp.dot(own, near, preferred_element_type=f32), 1e-12)
    tail = jnp.maximum(scale - square * lax.rsqrt(square), 0.0)
    return reduce_slope(tail * tail * tail, moments)


def reduce_slope(slope, moments):
    high = slope.astype(bf16)
    low = (slope - high.astype(f32)).astype(bf16)
    return lax.dot_general(moments, high, NT, preferred_element_type=f32) + lax.dot_general(
        moments, low, NT, preferred_element_type=f32
    )


def fold_parts(moments):
    return moments[0:8] + (moments[8:16] + moments[16:24])


def lane_sums(lanes):
    return jnp.concatenate(
        [
            jnp.sum(lanes[part : part + LANES].T, axis=0, keepdims=True)
            for part in range(0, lanes.shape[0], LANES)
        ],
        axis=1,
    )


def local_first_kernel(own_ref, near_ref, mass_ref, out_ref, density_ref):
    rows = own_ref.shape[0]
    own = own_ref[...]

    def step(index, carry):
        lanes, moments = carry
        at = pl.ds(pl.multiple_of(index * CHUNK, CHUNK), CHUNK)
        more_lanes, more = first_chunk(
            own, near_ref[:, at], mass_ref[:, at], near_ref[32:64, at]
        )
        return lanes + more_lanes, moments + more

    start = (jnp.zeros((rows, LANES), f32), jnp.zeros((32, rows), f32))
    lanes, moments = lax.fori_loop(0, near_ref.shape[1] // CHUNK, step, start)
    out_ref[...] = fold_parts(moments)
    density_ref[...] = lane_sums(lanes)


def local_second_kernel(own_ref, near_ref, scale_ref, moment_ref, out_ref):
    rows = own_ref.shape[0]
    own = own_ref[...]

    def step(index, moments):
        at = pl.ds(pl.multiple_of(index * CHUNK, CHUNK), CHUNK)
        return moments + second_chunk(
            own, near_ref[:, at], scale_ref[:, at], moment_ref[32:64, at]
        )

    moments = lax.fori_loop(
        0, near_ref.shape[1] // CHUNK, step, jnp.zeros((32, rows), f32)
    )
    out_ref[...] = fold_parts(moments)


def slot_place(slot, column_ref, place_ref, me, capacity, blocks, extra):
    sender = slot // capacity
    block = column_ref[sender * capacity + slot % capacity]
    apart = sender ^ me
    half = blocks // 2
    first = place_ref[0, apart]
    second = place_ref[1, apart]
    devices = place_ref.shape[1]
    row = jnp.where(
        block < half,
        first * (half + extra) + block,
        devices * (half + extra) + second * half + block - half,
    )
    return row, first * blocks + block


def fetch(pieces, gathered, semaphore):
    start = 0
    copies = []
    for number, piece in enumerate(pieces):
        count = piece.shape[0]
        copy = pltpu.make_async_copy(
            piece, gathered.at[pl.ds(start, count)], semaphore.at[number]
        )
        copy.start()
        copies.append(copy)
        start += count
    for copy in copies:
        copy.wait()


def remote_first_kernel(
    capacity,
    extra,
    slots_ref,
    column_ref,
    place_ref,
    me_ref,
    piece0,
    piece1,
    piece2,
    piece3,
    own_ref,
    fields_ref,
    centre_ref,
    entropy_ref,
    moments_ref,
    lanes_ref,
    density_ref,
    divergence_ref,
    scale_ref,
    gradient_ref,
    near2_ref,
    scale_row_ref,
    gathered,
    near,
    mass,
    semaphore,
):
    blocks = fields_ref.shape[0]
    partners = slots_ref.shape[1]
    fetch((piece0, piece1, piece2, piece3), gathered, semaphore)
    centre = centre_ref[...]
    me = me_ref[0]

    @pl.loop(0, blocks)
    def _(index):
        at = pl.ds(pl.multiple_of(index * LANES, LANES), LANES)
        for k in range(partners):
            row, _ = slot_place(
                slots_ref[index, k], column_ref, place_ref, me, capacity, blocks, extra
            )
            fields = gathered[row]
            value, more = moment_rows(*particle_rows(fields, centre))
            near[:, k * LANES : (k + 1) * LANES] = near_rows(value, more)
            mass[:, k * LANES : (k + 1) * LANES] = fields[6:7]
        lanes, moments = first_chunk(own_ref[at, :], near[...], mass[...], near[32:64, :])
        moments = fold_parts(moments) + moments_ref[:, at]
        total = lane_sums(lanes) + lanes_ref[:, at]
        fields = fields_ref[index]
        pos, vel, square, cross = particle_rows(fields, centre)
        smooth = fields[7:8]
        inverse = 1.0 / smooth
        cube = inverse * inverse * inverse
        density = total * cube * (kernel_norm / 256.0)
        factor = cube * inverse * inverse * (20.0 * kernel_norm / 64.0)
        approach = (
            cross * moments[6:7]
            + moments[7:8]
            - jnp.sum(vel * moments[0:3], axis=0, keepdims=True)
            - jnp.sum(pos * moments[3:6], axis=0, keepdims=True)
        )
        press = entropy_ref[pl.ds(index, 1), :] * inverse_cube_root(density)
        weight = (20.0 * kernel_norm) * fields[6:7] * press * cube * inverse * inverse
        root = inverse_cube_root(weight)
        scale = weight * root * root
        density_ref[pl.ds(index, 1), :] = density
        divergence_ref[pl.ds(index, 1), :] = factor * approach / density
        scale_ref[pl.ds(index, 1), :] = scale
        gradient = (pos * moments[6:7] - moments[0:3]) * (factor * press)
        gradient_ref[:, at] = jnp.concatenate(
            [gradient, jnp.zeros((5, LANES), f32)], axis=0
        )
        near2_ref[:, at] = near_rows(
            slope_rows(pos, square, scale, smooth), jnp.zeros((8, LANES), f32)
        )
        scale_row_ref[:, at] = scale


def inverse_cube_root(value):
    guess = jnp.exp(jnp.log(value) * (-1.0 / 3.0))
    guess = guess * (4.0 - value * guess * guess * guess) * (1.0 / 3.0)
    return guess * (4.0 - value * guess * guess * guess) * (1.0 / 3.0)


def remote_second_kernel(
    capacity,
    extra,
    slots_ref,
    column_ref,
    place_ref,
    me_ref,
    active_ref,
    piece0,
    piece1,
    piece2,
    piece3,
    scale0,
    scale1,
    own_ref,
    fields_ref,
    centre_ref,
    moments_ref,
    gradient_ref,
    out_ref,
    gathered,
    scales,
    near,
    moment,
    scale_row,
    semaphore,
    scale_semaphore,
):
    blocks = fields_ref.shape[0]
    partners = slots_ref.shape[1]
    fetch((piece0, piece1, piece2, piece3), gathered, semaphore)
    fetch((scale0, scale1), scales, scale_semaphore)
    centre = centre_ref[...]
    me = me_ref[0]

    @pl.loop(0, blocks)
    def _(index):
        at = pl.ds(pl.multiple_of(index * LANES, LANES), LANES)

        @pl.when(active_ref[index] > 0)
        def _():
            for k in range(partners):
                row, scale_at = slot_place(
                    slots_ref[index, k], column_ref, place_ref, me, capacity, blocks, extra
                )
                fields = gathered[row]
                scale = scales[pl.ds(scale_at, 1), :]
                pos, vel, square, cross = particle_rows(fields, centre)
                value = jnp.concatenate([pos, vel, jnp.ones_like(square), cross], axis=0)
                high, middle, low = split3(value)
                here = slice(k * LANES, (k + 1) * LANES)
                moment[:, here] = jnp.concatenate(
                    [high, middle, low, jnp.zeros_like(low)], axis=0
                ).astype(bf16)
                near[:, here] = near_rows(
                    slope_rows(pos, square, scale, fields[7:8]), jnp.zeros((8, LANES), f32)
                )
                scale_row[:, here] = scale
            moments = second_chunk(own_ref[at, :], near[...], scale_row[...], moment[...])
            moments = fold_parts(moments) + moments_ref[:, at]
            pos, _, _, _ = particle_rows(fields_ref[index], centre)
            out_ref[index] = gradient_ref[0:3, at] + (pos * moments[6:7] - moments[0:3])

        @pl.when(active_ref[index] <= 0)
        def _():
            out_ref[index] = jnp.zeros((3, LANES), f32)


def in_vmem(count):
    return [pl.BlockSpec(memory_space=pltpu.VMEM)] * count


def in_smem(count):
    return [pl.BlockSpec(memory_space=pltpu.SMEM)] * count


def in_any(count):
    return [pl.BlockSpec(memory_space=pl.ANY)] * count


def shape(*dims, dtype=f32):
    return jax.ShapeDtypeStruct(dims, dtype)


params = pltpu.CompilerParams(vmem_limit_bytes=48 * 2**20)


def prepare(fields):
    particles = fields.shape[0] * LANES
    return pl.pallas_call(
        prepare_kernel,
        out_shape=[
            shape(FEATS, particles, dtype=bf16),
            shape(particles, FEATS, dtype=bf16),
            shape(particles, FEATS, dtype=bf16),
            shape(1, particles),
            shape(8, LANES),
        ],
        in_specs=in_vmem(1),
        out_specs=in_vmem(5),
        compiler_params=params,
    )(fields)


def local_first(part, parts, own, near, mass):
    particles = near.shape[1]
    share = particles // parts
    steps = share // ROWS
    whole = lambda index: (0, 0)
    return pl.pallas_call(
        local_first_kernel,
        grid=(steps,),
        in_specs=[
            pl.BlockSpec((ROWS, FEATS), lambda index: (part * steps + index, 0)),
            pl.BlockSpec(near.shape, whole),
            pl.BlockSpec(mass.shape, whole),
        ],
        out_specs=[
            pl.BlockSpec((8, ROWS), lambda index: (0, index)),
            pl.BlockSpec((1, ROWS), lambda index: (0, index)),
        ],
        out_shape=[shape(8, share), shape(1, share)],
        cost_estimate=pl.CostEstimate(
            flops=share * particles * 400, bytes_accessed=2**20, transcendentals=0
        ),
        compiler_params=params,
    )(own, near, mass)


def local_second(part, parts, own, near, scale, moments):
    particles = near.shape[1]
    share = particles // parts
    steps = share // ROWS
    whole = lambda index: (0, 0)
    return pl.pallas_call(
        local_second_kernel,
        grid=(steps,),
        in_specs=[
            pl.BlockSpec((ROWS, FEATS), lambda index: (part * steps + index, 0)),
            pl.BlockSpec(near.shape, whole),
            pl.BlockSpec(scale.shape, whole),
            pl.BlockSpec(moments.shape, whole),
        ],
        out_specs=pl.BlockSpec((8, ROWS), lambda index: (0, index)),
        out_shape=shape(8, share),
        cost_estimate=pl.CostEstimate(
            flops=share * particles * 400, bytes_accessed=2**20, transcendentals=0
        ),
        compiler_params=params,
    )(own, near, scale, moments)


def doubling(value, order, devices):
    for number, bit in enumerate(order):
        other = lax.ppermute(value, "dom", [(i, i ^ bit) for i in range(devices)])
        if number == len(order) - 1:
            return value, other
        value = jnp.concatenate([value, other], axis=0)


def places(order, devices):
    table = np.zeros((devices,), np.int32)
    for apart in range(devices):
        table[apart] = sum(1 << k for k, bit in enumerate(order) if apart & bit)
    return table


def per_device(
    devices,
    positions,
    velocities,
    masses,
    smoothing,
    entropy,
    export_blocks,
    partner_slots,
    active,
):
    blocks = positions.shape[0]
    particles = blocks * LANES
    capacity = export_blocks.shape[2]
    half = blocks // 2
    me = lax.axis_index("dom")
    fields = jnp.concatenate(
        [positions, velocities, masses[:, None, :], smoothing[:, None, :]], axis=1
    )
    words = devices * capacity
    extra = -(-words // (8 * LANES))
    table = export_blocks.astype(f32).reshape(words)
    table = jnp.pad(table, (0, extra * 8 * LANES - words)).reshape(extra, 8, LANES)
    bits = [1 << k for k in reversed(range(devices.bit_length() - 1))]
    order0 = list(bits)
    order1 = list(bits)
    order1[-3:-1] = reversed(order1[-3:-1])
    first = doubling(jnp.concatenate([fields[:half], table], axis=0), order0, devices)
    second = doubling(fields[half:], order1, devices)
    pieces = (*first, *second)
    place0 = places(order0, devices)
    place = jnp.asarray(np.stack([place0, places(order1, devices)]))

    near, own, own2, mass, centre = prepare(fields)
    parts = 4
    sums = [local_first(part, parts, own, near, mass) for part in range(parts)]
    moments = jnp.concatenate([item[0] for item in sums], axis=1)
    lanes = jnp.concatenate([item[1] for item in sums], axis=1)

    step = half + extra
    tables = jnp.concatenate(
        [item.reshape(devices // 2, step, 8, LANES)[:, half:] for item in first], axis=0
    )
    tables = tables.reshape(devices, extra * 8 * LANES)[:, :words]
    tables = tables.reshape(devices, devices, capacity)
    column = lax.dynamic_index_in_dim(tables, me, axis=1, keepdims=False)
    senders = jnp.arange(devices, dtype=jnp.int32) ^ me
    column = column[jnp.asarray(place0)[senders]].astype(jnp.int32).reshape(words)
    me_array = me.astype(jnp.int32).reshape(1)

    rows = sum(piece.shape[0] for piece in pieces)
    partners = partner_slots.shape[1] * LANES
    density, divergence, scale, gradient, near2, scale_row = pl.pallas_call(
        functools.partial(remote_first_kernel, capacity, extra),
        out_shape=[
            shape(blocks, LANES),
            shape(blocks, LANES),
            shape(blocks, LANES),
            shape(8, particles),
            shape(FEATS, particles, dtype=bf16),
            shape(1, particles),
        ],
        in_specs=in_smem(4) + in_any(4) + in_vmem(6),
        out_specs=in_vmem(6),
        scratch_shapes=[
            pltpu.VMEM((rows, 8, LANES), f32),
            pltpu.VMEM((FEATS, partners), bf16),
            pltpu.VMEM((1, partners), f32),
            pltpu.SemaphoreType.DMA((4,)),
        ],
        compiler_params=params,
    )(
        partner_slots, column, place, me_array, *pieces, own, fields, centre, entropy,
        moments, lanes,
    )

    scales = doubling(scale, order0, devices)
    sums = [
        local_second(part, parts, own2, near2, scale_row, near) for part in range(parts)
    ]
    moments = jnp.concatenate(sums, axis=1)
    acceleration = pl.pallas_call(
        functools.partial(remote_second_kernel, capacity, extra),
        out_shape=shape(blocks, 3, LANES),
        in_specs=in_smem(5) + in_any(6) + in_vmem(5),
        out_specs=pl.BlockSpec(memory_space=pltpu.VMEM),
        scratch_shapes=[
            pltpu.VMEM((rows, 8, LANES), f32),
            pltpu.VMEM((devices * blocks, LANES), f32),
            pltpu.VMEM((FEATS, partners), bf16),
            pltpu.VMEM((32, partners), bf16),
            pltpu.VMEM((1, partners), f32),
            pltpu.SemaphoreType.DMA((4,)),
            pltpu.SemaphoreType.DMA((2,)),
        ],
        compiler_params=params,
    )(
        partner_slots, column, place, me_array, active, *pieces, *scales, own2, fields,
        centre, moments, gradient,
    )
    return (density, divergence, acceleration)


def solution(mesh):
    in_specs = (
        P("dom", None, None),
        P("dom", None, None),
        P("dom", None),
        P("dom", None),
        P("dom", None),
        P("dom", None, None),
        P("dom", None),
        P("dom"),
    )
    out_specs = (P("dom", None), P("dom", None), P("dom", None, None))
    return jax.shard_map(
        functools.partial(per_device, mesh.shape["dom"]),
        mesh=mesh,
        in_specs=in_specs,
        out_specs=out_specs,
        check_vma=False,
    )
```

```python
import functools

import jax
import jax.numpy as jnp
import numpy as np
from jax import lax
from jax.experimental import pallas as pl
from jax.experimental.pallas import tpu as pltpu
from jax.sharding import PartitionSpec as P

kernel_norm = 3.3422538049298023
LANES = 128
FEATS = 48
TILE = 256
bf16 = jnp.bfloat16
f32 = jnp.float32


def split3(value):
    high = value.astype(bf16).astype(f32)
    rest = value - high
    middle = rest.astype(bf16).astype(f32)
    return high, middle, rest - middle


def near_rows(four, last):
    high, middle, low = split3(jnp.concatenate([four, four], axis=0))
    upper = lax.broadcasted_iota(jnp.int32, high.shape, 0) < 4
    mixed = jnp.where(upper, high, middle)
    blank = jnp.zeros((FEATS - 35, LANES), f32)
    rows = jnp.concatenate([high, middle, low, mixed, *last, blank], axis=0)
    return rows.T.astype(bf16)


def own_rows(four, last):
    high, middle, low = split3(four)
    pair = [high, middle]
    blank = jnp.zeros((FEATS - 35, LANES), f32)
    rows = pair * 3 + [low, low, *last, blank]
    return jnp.concatenate(rows, axis=0).astype(bf16)


def split_rows(value):
    parts = list(split3(value))
    if value.shape[0] % 8 == 0:
        parts.append(jnp.zeros_like(value))
    else:
        parts.append(jnp.zeros((16 - 3 * value.shape[0], LANES), f32))
    return jnp.concatenate(parts, axis=0).astype(bf16)


def fold_rows(moments, count):
    return moments[0:count] + (moments[count : 2 * count] + moments[2 * count : 3 * count])


def particle_rows(fields, centre):
    shifted = fields - centre
    pos = shifted[0:3]
    vel = shifted[3:6]
    square = jnp.sum(pos * pos, axis=0, keepdims=True)
    return pos, vel, square


def first_near(fields, centre):
    pos, vel, square = particle_rows(fields, centre)
    one = jnp.ones_like(square)
    cross = jnp.sum(pos * vel, axis=0, keepdims=True)
    near = near_rows(jnp.concatenate([pos, square], axis=0), [one] * 3)
    moments = split_rows(jnp.concatenate([pos, vel, one, cross], axis=0))
    return near, moments


def second_near(fields, centre, weight):
    pos, _, square = particle_rows(fields, centre)
    inverse = 1.0 / fields[7:8]
    inverse = inverse * inverse
    last = split3(square * inverse)
    near = near_rows(jnp.concatenate([pos * inverse, inverse], axis=0), last)
    moments = split_rows(jnp.concatenate([pos * weight, weight], axis=0))
    return near, moments


def spread(row):
    return jnp.broadcast_to(row, (LANES, LANES)).T


def prepare_kernel(fields_ref, near_ref, moment_ref, mass_ref, own_ref, own2_ref, centre_ref):
    blocks = fields_ref.shape[0]
    total = jnp.sum(fields_ref[...], axis=0)
    mean = jnp.sum(total, axis=1, keepdims=True) / (blocks * LANES)
    rows = lax.broadcasted_iota(jnp.int32, (8, LANES), 0)
    centre = jnp.where(rows < 6, jnp.broadcast_to(mean, (8, LANES)), 0.0)
    centre_ref[...] = centre

    def block(index):
        fields = fields_ref[index]
        at = pl.ds(pl.multiple_of(index * LANES, LANES), LANES)
        near_ref[at, :], moment_ref[:, at] = first_near(fields, centre)
        mass_ref[at, :] = spread(fields[6:7])
        pos, _, square = particle_rows(fields, centre)
        smooth = fields[7:8]
        sigma = 16.0 / (smooth * smooth)
        four = jnp.concatenate([pos * (-2.0 * sigma), sigma], axis=0)
        own_ref[:, at] = own_rows(four, split3(square * sigma))
        one = jnp.ones_like(square)
        four = jnp.concatenate([pos * -2.0, square], axis=0)
        own2_ref[:, at] = own_rows(four, [one] * 3)

    @pl.loop(0, blocks // 4)
    def _(group):
        for part in range(4):
            block(group * 4 + part)


def halves(slope):
    high = slope.astype(bf16)
    low = (slope - high.astype(f32)).astype(bf16)
    return jnp.concatenate([high, low], axis=0)


def pair_sums(own, near_ref, moment_ref, mass_ref, start, chunk, steps):
    width = own.shape[1]
    dense = None
    total = None

    def place(step):
        if isinstance(start, int):
            return pl.ds(start + step * chunk, chunk)
        return pl.ds(pl.multiple_of(start + step * chunk, chunk), chunk)

    def product(step):
        return jnp.dot(near_ref[place(step), :], own, preferred_element_type=f32)

    def moment(step, slope):
        fields = moment_ref[:, place(step)]
        both = jnp.concatenate([fields, fields], axis=1)
        return jnp.dot(both, slope, preferred_element_type=f32)

    square = product(0)
    slope = None
    for step in range(steps):
        following = product(step + 1) if step + 1 < steps else None
        square = jnp.maximum(square, 1e-12)
        radius = square * lax.rsqrt(square)
        if mass_ref is None:
            tail = jnp.maximum(1.0 - radius, 0.0)
            cube = tail * tail * tail
        else:
            mass = mass_ref[place(step), :]
            mass = jnp.concatenate([mass] * (width // LANES), axis=1)
            tail = jnp.maximum(4.0 - radius, 0.0)
            cube = tail * tail * tail * mass
            value = cube * (tail * (5.0 - tail))
            value = jnp.sum(value.reshape(chunk // 8, 8, width), axis=0)
            dense = value if dense is None else dense + value
        if slope is not None:
            more = moment(step - 1, slope)
            total = more if total is None else total + more
        slope = halves(cube)
        square = following
    more = moment(steps - 1, slope)
    total = more if total is None else total + more
    return dense, total


def local_first_kernel(own_ref, near_ref, moment_ref, mass_ref, *refs):
    out_ref, dense_ref = refs[-2:]
    own = own_ref[...]
    width = own.shape[1]
    particles = near_ref.shape[0]
    chunk, steps = 256, 16
    steps = min(steps, particles // chunk)

    def step(index, carry):
        dense, total = pair_sums(
            own, near_ref, moment_ref, mass_ref, index * (chunk * steps), chunk, steps
        )
        return carry[0] + dense, carry[1] + total

    zero = (jnp.zeros((8, width), f32), jnp.zeros((32, width), f32))
    dense, total = lax.fori_loop(0, particles // (chunk * steps), step, zero)
    out_ref[...] = fold_rows(total, 8)
    dense_ref[...] = dense


def local_second_kernel(own_ref, near_ref, moment_ref, *refs):
    out_ref = refs[-1]
    own = own_ref[...]
    width = own.shape[1]
    particles = near_ref.shape[0]
    chunk, steps = 256, 16
    steps = min(steps, particles // chunk)

    def step(index, carry):
        _, total = pair_sums(
            own, near_ref, moment_ref, None, index * (chunk * steps), chunk, steps
        )
        return carry + total

    zero = jnp.zeros((16, width), f32)
    total = lax.fori_loop(0, particles // (chunk * steps), step, zero)
    out_ref[...] = jnp.concatenate([fold_rows(total, 4), jnp.zeros((4, width), f32)], axis=0)


def slot_place(slot, tables_ref, place_ref, me, capacity, blocks, extra):
    sender = slot // capacity
    apart = sender ^ me
    first = place_ref[0, apart]
    second = place_ref[1, apart]
    block = tables_ref[first, (me * capacity) % LANES + slot % capacity]
    half = blocks // 2
    devices = place_ref.shape[1]
    row = jnp.where(
        block < half,
        first * (half + extra) + block,
        devices * (half + extra) + second * half + block - half,
    )
    return row, first * blocks + block


def fetch(pieces, gathered, semaphore):
    start = 0
    copies = []
    for number, piece in enumerate(pieces):
        count = piece.shape[0]
        copy = pltpu.make_async_copy(
            piece, gathered.at[pl.ds(start, count)], semaphore.at[number]
        )
        copy.start()
        copies.append(copy)
        start += count
    return copies


def in_turn(blocks, build, sums):
    build(0, 0)

    @pl.loop(0, blocks // 2)
    def _(pair):
        build(pair * 2 + 1, 1)
        sums(pair * 2, 0)
        build(jnp.minimum(pair * 2 + 2, blocks - 1), 0)
        sums(pair * 2 + 1, 1)


def remote_first_kernel(
    capacity,
    extra,
    slots_ref,
    tables_ref,
    place_ref,
    me_ref,
    piece0,
    piece1,
    piece2,
    piece3,
    own_ref,
    fields_ref,
    centre_ref,
    entropy_ref,
    moments_ref,
    dense_ref,
    density_ref,
    divergence_ref,
    weight_ref,
    gradient_ref,
    gathered,
    near0,
    near1,
    moment0,
    moment1,
    mass0,
    mass1,
    sums_ref,
    semaphore,
):
    blocks = fields_ref.shape[0]
    partners = slots_ref.shape[1]
    copies = fetch((piece0, piece1, piece2, piece3), gathered, semaphore)
    for copy in copies:
        copy.wait()
    centre = centre_ref[...]
    me = me_ref[0]
    sides = ((near0, moment0, mass0), (near1, moment1, mass1))

    def build(index, side):
        near, moment, mass = sides[side]
        for k in range(partners):
            row, _ = slot_place(
                slots_ref[index, k], tables_ref, place_ref, me, capacity, blocks, extra
            )
            fields = gathered[row]
            at = slice(k * LANES, (k + 1) * LANES)
            near[at, :], moment[:, at] = first_near(fields, centre)
            mass[at, :] = spread(fields[6:7])

    def sums(index, side):
        near, moment, mass = sides[side]
        at = pl.ds(pl.multiple_of(index * LANES, LANES), LANES)
        dense, total = pair_sums(
            own_ref[:, at], near, moment, mass, 0, 512, partners * LANES // 512
        )
        sums_ref[index, 0:8, :] = fold_rows(total, 8) + moments_ref[:, at]
        sums_ref[index, 8:16, :] = dense + dense_ref[:, at]

    in_turn(blocks, build, sums)
    total = sums_ref[:, 8, :]
    for row in range(9, 16):
        total = total + sums_ref[:, row, :]
    moments = [sums_ref[:, row, :] for row in range(8)]
    own = [fields_ref[:, row, :] - centre[row : row + 1, :] for row in range(8)]
    inverse = 1.0 / own[7]
    cube = inverse * inverse * inverse
    density = total * cube * (kernel_norm / 256.0)
    factor = cube * inverse * inverse * (20.0 * kernel_norm / 64.0)
    cross = own[0] * own[3] + own[1] * own[4] + own[2] * own[5]
    approach = cross * moments[6] + moments[7]
    for row in range(3):
        approach = approach - own[row + 3] * moments[row] - own[row] * moments[row + 3]
    press = entropy_ref[...] * inverse_cube_root(density)
    density_ref[...] = density
    divergence_ref[...] = factor * approach / density
    weight_ref[...] = (20.0 * kernel_norm) * own[6] * press * (cube * inverse * inverse)
    for row in range(3):
        gradient = (own[row] * moments[6] - moments[row]) * (factor * press)
        gradient_ref[row] = gradient


def inverse_cube_root(value):
    guess = jnp.exp(jnp.log(value) * (-1.0 / 3.0))
    guess = guess * (4.0 - value * guess * guess * guess) * (1.0 / 3.0)
    return guess * (4.0 - value * guess * guess * guess) * (1.0 / 3.0)


def prepare_second_kernel(fields_ref, centre_ref, weight_ref, near_ref, moment_ref):
    blocks = fields_ref.shape[0]
    centre = centre_ref[...]

    @pl.loop(0, blocks // 4)
    def _(group):
        for part in range(4):
            index = group * 4 + part
            at = pl.ds(pl.multiple_of(index * LANES, LANES), LANES)
            near_ref[at, :], moment_ref[:, at] = second_near(
                fields_ref[index], centre, weight_ref[pl.ds(index, 1), :]
            )


def remote_second_kernel(
    capacity,
    extra,
    slots_ref,
    tables_ref,
    place_ref,
    me_ref,
    active_ref,
    piece0,
    piece1,
    piece2,
    piece3,
    weight0,
    weight1,
    own_ref,
    fields_ref,
    centre_ref,
    moments_ref,
    gradient_ref,
    out_ref,
    gathered,
    weights,
    near0,
    near1,
    moment0,
    moment1,
    semaphore,
    weight_semaphore,
):
    blocks = fields_ref.shape[0]
    partners = slots_ref.shape[1]
    copies = fetch((piece0, piece1, piece2, piece3), gathered, semaphore)
    copies += fetch((weight0, weight1), weights, weight_semaphore)
    for copy in copies:
        copy.wait()
    centre = centre_ref[...]
    me = me_ref[0]
    sides = ((near0, moment0), (near1, moment1))

    def build(index, side):
        near, moment = sides[side]
        for k in range(partners):
            row, weight_row = slot_place(
                slots_ref[index, k], tables_ref, place_ref, me, capacity, blocks, extra
            )
            at = slice(k * LANES, (k + 1) * LANES)
            near[at, :], moment[:, at] = second_near(
                gathered[row], centre, weights[pl.ds(weight_row, 1), :]
            )

    def sums(index, side):
        near, moment = sides[side]
        at = pl.ds(pl.multiple_of(index * LANES, LANES), LANES)
        _, total = pair_sums(
            own_ref[:, at], near, moment, None, 0, 512, partners * LANES // 512
        )
        total = fold_rows(total, 4) + moments_ref[0:4, at]
        pos, _, _ = particle_rows(fields_ref[index], centre)
        out = gradient_ref[:, index, :] + (pos * total[3:4] - total[0:3])
        out_ref[index] = jnp.where(active_ref[index] > 0, out, 0.0)

    in_turn(blocks, build, sums)


def join_kernel(*refs):
    count = (len(refs) - 1) // 3
    copies = []
    for number in range(count):
        out = refs[2 * count + number]
        start = 0
        for part in range(2):
            piece = refs[2 * number + part]
            copy = pltpu.make_async_copy(
                piece, out.at[pl.ds(start, piece.shape[0])], refs[-1].at[2 * number + part]
            )
            copy.start()
            copies.append(copy)
            start += piece.shape[0]
    for copy in copies:
        copy.wait()


def in_vmem(count):
    return [pl.BlockSpec(memory_space=pltpu.VMEM)] * count


def in_smem(count):
    return [pl.BlockSpec(memory_space=pltpu.SMEM)] * count


def in_any(count):
    return [pl.BlockSpec(memory_space=pl.ANY)] * count


def shape(*dims, dtype=f32):
    return jax.ShapeDtypeStruct(dims, dtype)


params = pltpu.CompilerParams(vmem_limit_bytes=48 * 2**20)


def join(*pairs):
    flat = [item for pair in pairs for item in pair]
    outs = [shape(2 * pair[0].shape[0], *pair[0].shape[1:]) for pair in pairs]
    return pl.pallas_call(
        join_kernel,
        out_shape=outs,
        in_specs=in_any(len(flat)),
        out_specs=in_any(len(outs)),
        scratch_shapes=[pltpu.SemaphoreType.DMA((len(flat),))],
        compiler_params=params,
    )(*flat)


def prepare(fields):
    particles = fields.shape[0] * LANES
    return pl.pallas_call(
        prepare_kernel,
        out_shape=[
            shape(particles, FEATS, dtype=bf16),
            shape(32, particles, dtype=bf16),
            shape(particles, LANES),
            shape(FEATS, particles, dtype=bf16),
            shape(FEATS, particles, dtype=bf16),
            shape(8, LANES),
        ],
        in_specs=in_vmem(1),
        out_specs=in_vmem(6),
        compiler_params=params,
    )(fields)


def prepare_second(fields, centre, weight):
    particles = fields.shape[0] * LANES
    return pl.pallas_call(
        prepare_second_kernel,
        out_shape=[
            shape(particles, FEATS, dtype=bf16),
            shape(16, particles, dtype=bf16),
        ],
        in_specs=in_vmem(3),
        out_specs=in_vmem(2),
        compiler_params=params,
    )(fields, centre, weight)


def local_pass(kernel, first, count, own, whole, sums):
    particles = own.shape[1]
    fixed = lambda index: (0, 0)
    here = lambda index: (0, first + index)
    height = 2 if kernel is local_first_kernel else 1
    outs = [shape(8, particles)] * height
    aliases = {}
    operands = [own, *whole]
    in_specs = [pl.BlockSpec((FEATS, TILE), here)]
    in_specs += [pl.BlockSpec(item.shape, fixed) for item in whole]
    if sums is not None:
        aliases = {len(operands) + number: number for number in range(height)}
        operands += list(sums)
        in_specs += in_any(height)
    return pl.pallas_call(
        kernel,
        grid=(count,),
        in_specs=in_specs,
        out_specs=[pl.BlockSpec((8, TILE), here)] * height,
        out_shape=outs,
        input_output_aliases=aliases,
        cost_estimate=pl.CostEstimate(
            flops=count * TILE * particles * 2000, bytes_accessed=2**20, transcendentals=0
        ),
        compiler_params=params,
    )(*operands)


def swap(value, bit, devices):
    return lax.ppermute(value, "dom", [(i, i ^ bit) for i in range(devices)])


def places(order, devices):
    table = np.zeros((devices,), np.int32)
    for apart in range(devices):
        table[apart] = sum(1 << k for k, bit in enumerate(order) if apart & bit)
    return table


def shares(tiles, stages):
    cuts = [round(tiles * k / stages) for k in range(stages + 1)]
    return list(zip(cuts[:-1], cuts[1:]))


def per_device(
    devices,
    positions,
    velocities,
    masses,
    smoothing,
    entropy,
    export_blocks,
    partner_slots,
    active,
):
    blocks = positions.shape[0]
    particles = blocks * LANES
    capacity = export_blocks.shape[2]
    half = blocks // 2
    me = lax.axis_index("dom")
    fields = jnp.concatenate(
        [positions, velocities, masses[:, None, :], smoothing[:, None, :]], axis=1
    )
    words = devices * capacity
    extra = -(-words // (8 * LANES))
    table = export_blocks.astype(f32).reshape(words)
    table = jnp.pad(table, (0, extra * 8 * LANES - words)).reshape(extra, 8, LANES)
    bits = [1 << k for k in reversed(range(devices.bit_length() - 1))]
    order0 = list(bits)
    order1 = list(bits)
    order1[-3:-1] = reversed(order1[-3:-1])
    place = jnp.asarray(np.stack([places(order0, devices), places(order1, devices)]))
    tiles = particles // TILE
    stages = len(bits)

    near, moment, mass, own, own2, centre = prepare(fields)
    first = jnp.concatenate([fields[:half], table], axis=0)
    second = fields[half:]
    sums = None
    for number, (start, stop) in enumerate(shares(tiles, stages)):
        first_in = swap(first, order0[number], devices)
        second_in = swap(second, order1[number], devices)
        if stop > start:
            sums = local_pass(
                local_first_kernel, start, stop - start, own, (near, moment, mass), sums
            )
        if number < stages - 1:
            first, first_in, second, second_in, near, sums = lax.optimization_barrier(
                (first, first_in, second, second_in, near, sums)
            )
            first, second = join((first, first_in), (second, second_in))
    pieces = (first, first_in, second, second_in)

    step = half + extra
    line = (me * capacity) // LANES
    tables = [
        lax.dynamic_slice(
            item.reshape(devices // 2, step, 8, LANES),
            (0, half + line // 8, line % 8, 0),
            (devices // 2, 1, 1, LANES),
        ).reshape(devices // 2, LANES)
        for item in (first, first_in)
    ]
    tables = jnp.concatenate(tables, axis=0).astype(jnp.int32)
    me_array = me.astype(jnp.int32).reshape(1)

    rows = sum(piece.shape[0] for piece in pieces)
    partners = partner_slots.shape[1] * LANES
    near_side = [pltpu.VMEM((partners, FEATS), bf16)] * 2
    density, divergence, weight, gradient = pl.pallas_call(
        functools.partial(remote_first_kernel, capacity, extra),
        out_shape=[
            shape(blocks, LANES),
            shape(blocks, LANES),
            shape(blocks, LANES),
            shape(3, blocks, LANES),
        ],
        in_specs=in_smem(4) + in_any(4) + in_vmem(6),
        out_specs=in_vmem(4),
        scratch_shapes=[
            pltpu.VMEM((rows, 8, LANES), f32),
            *near_side,
            pltpu.VMEM((32, partners), bf16),
            pltpu.VMEM((32, partners), bf16),
            pltpu.VMEM((partners, LANES), f32),
            pltpu.VMEM((partners, LANES), f32),
            pltpu.VMEM((blocks, 16, LANES), f32),
            pltpu.SemaphoreType.DMA((4,)),
        ],
        compiler_params=params,
    )(
        partner_slots, tables, place, me_array, *pieces, own, fields, centre, entropy, *sums
    )

    near2, moment2 = prepare_second(fields, centre, weight)
    sums = None
    for number, (start, stop) in enumerate(shares(tiles, stages)):
        weight_in = swap(weight, order0[number], devices)
        if stop > start:
            sums = local_pass(
                local_second_kernel, start, stop - start, own2, (near2, moment2), sums
            )
        if number < stages - 1:
            weight, weight_in, near2, sums = lax.optimization_barrier(
                (weight, weight_in, near2, sums)
            )
            (weight,) = join((weight, weight_in))

    acceleration = pl.pallas_call(
        functools.partial(remote_second_kernel, capacity, extra),
        out_shape=shape(blocks, 3, LANES),
        in_specs=in_smem(5) + in_any(6) + in_vmem(5),
        out_specs=pl.BlockSpec(memory_space=pltpu.VMEM),
        scratch_shapes=[
            pltpu.VMEM((rows, 8, LANES), f32),
            pltpu.VMEM((devices * blocks, LANES), f32),
            *near_side,
            pltpu.VMEM((16, partners), bf16),
            pltpu.VMEM((16, partners), bf16),
            pltpu.SemaphoreType.DMA((4,)),
            pltpu.SemaphoreType.DMA((2,)),
        ],
        compiler_params=params,
    )(
        partner_slots, tables, place, me_array, active, *pieces, weight, weight_in, own2,
        fields, centre, *sums, gradient,
    )
    return (density, divergence, acceleration)


def solution(mesh):
    in_specs = (
        P("dom", None, None),
        P("dom", None, None),
        P("dom", None),
        P("dom", None),
        P("dom", None),
        P("dom", None, None),
        P("dom", None),
        P("dom"),
    )
    out_specs = (P("dom", None), P("dom", None), P("dom", None, None))
    return jax.shard_map(
        functools.partial(per_device, mesh.shape["dom"]),
        mesh=mesh,
        in_specs=in_specs,
        out_specs=out_specs,
        check_vma=False,
    )
```

```python
import functools

import jax
import jax.numpy as jnp
import numpy as np
from jax import lax
from jax.experimental import pallas as pl
from jax.experimental.pallas import tpu as pltpu
from jax.sharding import PartitionSpec as P

kernel_norm = 3.3422538049298023
LANES = 128
FEATS = 48
TILE = 256
PIECES = 8
bf16 = jnp.bfloat16
f32 = jnp.float32


def split3(value):
    high = value.astype(bf16).astype(f32)
    rest = value - high
    middle = rest.astype(bf16).astype(f32)
    return high, middle, rest - middle


def near_rows(four, last):
    high, middle, low = split3(jnp.concatenate([four, four], axis=0))
    upper = lax.broadcasted_iota(jnp.int32, high.shape, 0) < 4
    mixed = jnp.where(upper, high, middle)
    blank = jnp.zeros((FEATS - 40, LANES), f32)
    return jnp.concatenate([high, middle, low, mixed, *last, blank], axis=0)


def own_rows(four, last):
    high, middle, low = split3(four)
    pair = [high, middle]
    blank = jnp.zeros((FEATS - 35, LANES), f32)
    rows = pair * 3 + [low, low, *last, blank]
    return jnp.concatenate(rows, axis=0).astype(bf16)


def split_rows(value):
    parts = list(split3(value))
    if value.shape[0] % 8 == 0:
        parts.append(jnp.zeros_like(value))
    else:
        parts.append(jnp.zeros((16 - 3 * value.shape[0], LANES), f32))
    return jnp.concatenate(parts, axis=0).astype(bf16)


def fold_rows(moments, count):
    return moments[0:count] + (moments[count : 2 * count] + moments[2 * count : 3 * count])


def particle_rows(fields, centre):
    shifted = fields - centre
    pos = shifted[0:3]
    vel = shifted[3:6]
    square = jnp.sum(pos * pos, axis=0, keepdims=True)
    return pos, vel, square


def first_near(fields, centre):
    pos, vel, square = particle_rows(fields, centre)
    one = jnp.ones_like(square)
    cross = jnp.sum(pos * vel, axis=0, keepdims=True)
    last = [one, one, one, fields[6:7], jnp.zeros((4, LANES), f32)]
    near = near_rows(jnp.concatenate([pos, square], axis=0), last)
    moments = split_rows(jnp.concatenate([pos, vel, one, cross], axis=0))
    return near, moments


def second_near(fields, centre, weight):
    pos, _, square = particle_rows(fields, centre)
    inverse = 1.0 / fields[7:8]
    inverse = inverse * inverse
    last = [*split3(square * inverse), jnp.zeros((5, LANES), f32)]
    near = near_rows(jnp.concatenate([pos * inverse, inverse], axis=0), last)
    moments = split_rows(jnp.concatenate([pos * weight, weight], axis=0))
    return near, moments


MASS_ROW = 35


def spread(turned, column):
    return jnp.broadcast_to(turned[:, column : column + 1], (LANES, LANES))


def assemble_kernel(*refs):
    inputs, (fields_ref, first_ref, second_ref), buffers = refs[:5], refs[5:8], refs[8:13]
    semaphore = refs[13]
    copies = [
        pltpu.make_async_copy(source, target, semaphore.at[number])
        for number, (source, target) in enumerate(zip(inputs, buffers))
    ]
    for copy in copies:
        copy.start()
    for copy in copies:
        copy.wait()
    pos_ref, vel_ref, mass_ref, smooth_ref, table_ref = buffers
    blocks = fields_ref.shape[0]
    half = second_ref.shape[0]
    fields_ref[:, 0:3, :] = pos_ref[...]
    fields_ref[:, 3:6, :] = vel_ref[...]
    fields_ref[:, 6, :] = mass_ref[...]
    fields_ref[:, 7, :] = smooth_ref[...]
    first_ref[0 : blocks - half] = fields_ref[0 : blocks - half]
    second_ref[...] = fields_ref[blocks - half :]
    table = table_ref[0].astype(f32)
    devices, capacity = table.shape
    lines = [table[row : row + 8] for row in range(0, devices, 8)]
    each = LANES // capacity
    for number in range(0, len(lines), each):
        line = jnp.concatenate(lines[number : number + each], axis=1)
        first_ref[blocks - half + number // each, :, 0 : line.shape[1]] = line


def prepare_kernel(fields_ref, near_ref, moment_ref, mass_ref, own_ref, centre_ref):
    blocks = fields_ref.shape[0]
    total = jnp.sum(fields_ref[...], axis=0)
    mean = jnp.sum(total, axis=1, keepdims=True) / (blocks * LANES)
    rows = lax.broadcasted_iota(jnp.int32, (8, LANES), 0)
    centre = jnp.where(rows < 6, jnp.broadcast_to(mean, (8, LANES)), 0.0)
    centre_ref[...] = centre
    mass_ref[...] = fields_ref[:, 6, :].T

    @pl.loop(0, blocks // 4)
    def _(group):
        for part in range(4):
            index = group * 4 + part
            fields = fields_ref[index]
            at = pl.ds(pl.multiple_of(index * LANES, LANES), LANES)
            near, moment_ref[:, at] = first_near(fields, centre)
            near_ref[at, :] = near.T.astype(bf16)
            pos, _, square = particle_rows(fields, centre)
            smooth = fields[7:8]
            sigma = 16.0 / (smooth * smooth)
            four = jnp.concatenate([pos * (-2.0 * sigma), sigma], axis=0)
            own_ref[:, at] = own_rows(four, split3(square * sigma))


def halves(slope):
    high = slope.astype(bf16)
    low = (slope - high.astype(f32)).astype(bf16)
    return jnp.concatenate([high, low], axis=0)


def pair_sums(own, near_ref, moment_ref, mass_of, chunk):
    width = own.shape[1]
    steps = near_ref.shape[0] // chunk
    dense = None
    total = None

    def place(step):
        return pl.ds(step * chunk, chunk)

    def product(step):
        return jnp.dot(near_ref[place(step), :], own, preferred_element_type=f32)

    def moment(step, slope):
        fields = moment_ref[:, place(step)]
        both = jnp.concatenate([fields, fields], axis=1)
        return jnp.dot(both, slope, preferred_element_type=f32)

    square = product(0)
    slope = None
    for step in range(steps):
        following = product(step + 1) if step + 1 < steps else None
        square = jnp.maximum(square, 1e-12)
        radius = square * lax.rsqrt(square)
        if mass_of is None:
            tail = jnp.maximum(1.0 - radius, 0.0)
            cube = tail * tail * tail
        else:
            mass = mass_of(step)
            tail = jnp.maximum(4.0 - radius, 0.0)
            cube = tail * tail * tail * mass
            value = cube * (tail * (5.0 - tail))
            value = jnp.sum(value.reshape(chunk // 8, 8, width), axis=0)
            dense = value if dense is None else dense + value
        if slope is not None:
            more = moment(step - 1, slope)
            total = more if total is None else total + more
        slope = halves(cube)
        square = following
    more = moment(steps - 1, slope)
    total = more if total is None else total + more
    return dense, total


def local_first_kernel(own_ref, near_ref, moment_ref, mass_ref, *refs):
    out_ref, dense_ref = refs[-2:]
    own = own_ref[...]
    mass = mass_ref[...]
    chunk = 2 * LANES

    def mass_of(step):
        column = jnp.concatenate(
            [spread(mass, block) for block in (2 * step, 2 * step + 1)], axis=0
        )
        return jnp.concatenate([column] * (own.shape[1] // LANES), axis=1)

    dense, total = pair_sums(own, near_ref, moment_ref, mass_of, chunk)
    out_ref[...] = fold_rows(total, 8)
    dense_ref[...] = dense


def local_second_kernel(own_ref, near_ref, moment_ref, *refs):
    out_ref = refs[-1]
    own = own_ref[...]
    _, total = pair_sums(own, near_ref, moment_ref, None, 2 * LANES)
    blank = jnp.zeros((4, own.shape[1]), f32)
    out_ref[...] = jnp.concatenate([fold_rows(total, 4), blank], axis=0)


def diagonal(own):
    blank = jnp.zeros((FEATS, LANES), bf16)
    upper = jnp.concatenate([own[:, 0:LANES], blank], axis=1)
    lower = jnp.concatenate([blank, own[:, LANES:]], axis=1)
    return jnp.concatenate([upper, lower], axis=0)


def slot_place(slot, tables_ref, place_ref, me, capacity, blocks, extra):
    sender = slot // capacity
    apart = sender ^ me
    first = place_ref[0, apart]
    second = place_ref[1, apart]
    block = tables_ref[first, (me // 8 * capacity) % LANES + slot % capacity]
    half = blocks // 2
    devices = place_ref.shape[1]
    row = jnp.where(
        block < half,
        first * (half + extra) + block,
        devices * (half + extra) + second * half + block - half,
    )
    return row, first * blocks + block


def fetch(pieces, gathered, semaphore):
    start = 0
    copies = []
    for number, piece in enumerate(pieces):
        count = piece.shape[0]
        copy = pltpu.make_async_copy(
            piece, gathered.at[pl.ds(start, count)], semaphore.at[number]
        )
        copy.start()
        copies.append(copy)
        start += count
    return copies


def in_turn(pairs, build, sums):
    build(0, 0)

    @pl.loop(0, pairs // 2)
    def _(step):
        build(step * 2 + 1, 1)
        sums(step * 2, 0)
        build(jnp.minimum(step * 2 + 2, pairs - 1), 0)
        sums(step * 2 + 1, 1)


def own_tables(gathered, line_ref, tables_ref, semaphore, place, me, capacity):
    step, half, extra = place
    line = me // 8 * capacity // LANES
    devices = line_ref.shape[0]
    chosen = lax.broadcasted_iota(jnp.int32, (8, LANES), 0) == me % 8
    for device in range(devices):
        block = gathered[device * step + half + line]
        row = jnp.sum(jnp.where(chosen, block, 0.0), axis=0, keepdims=True)
        line_ref[device : device + 1, :] = row.astype(jnp.int32)
    copy = pltpu.make_async_copy(line_ref, tables_ref, semaphore)
    copy.start()
    copy.wait()


def remote_first_kernel(
    capacity,
    extra,
    place_ref,
    me_ref,
    slots_hbm,
    *refs,
):
    pieces, refs = refs[:PIECES], refs[PIECES:]
    own_ref, fields_ref, centre_ref, entropy_ref, moments_ref, dense_ref = refs[:6]
    density_ref, divergence_ref, weight_ref, gradient_ref, line_ref = refs[6:11]
    gathered, tables_ref, near0, near1, moment0, moment1, mass0, mass1 = refs[11:19]
    sums_ref, slots_ref, semaphore, table_semaphore, slots_semaphore = refs[19:]
    blocks = fields_ref.shape[0]
    partners = slots_ref.shape[1]
    copies = fetch((slots_hbm,), slots_ref, slots_semaphore)
    copies += fetch(pieces, gathered, semaphore)
    for copy in copies:
        copy.wait()
    centre = centre_ref[...]
    me = me_ref[0]
    half = blocks // 2
    place = (half + extra, half, extra)
    own_tables(gathered, line_ref, tables_ref, table_semaphore, place, me, capacity)
    sides = ((near0, moment0, mass0), (near1, moment1, mass1))

    def build(pair, side):
        near, moment, mass = sides[side]
        for k in range(partners):
            at = slice(k * LANES, (k + 1) * LANES)
            rows = []
            for odd in range(2):
                row, _ = slot_place(
                    slots_ref[pair * 2 + odd, k],
                    tables_ref, place_ref, me, capacity, blocks, extra,
                )
                values, moments = first_near(gathered[row], centre)
                rows.append(values)
                moment[odd * 32 : odd * 32 + 32, at] = moments
            turned = jnp.concatenate(rows, axis=0).T
            near[at, :] = turned.astype(bf16)
            for odd in range(2):
                mass[at, odd * LANES : (odd + 1) * LANES] = spread(turned, odd * FEATS + MASS_ROW)

    def sums(pair, side):
        near, moment, mass = sides[side]
        at = pl.ds(pl.multiple_of(pair * 2 * LANES, 2 * LANES), 2 * LANES)
        dense, total = pair_sums(
            diagonal(own_ref[:, at]), near, moment, lambda step: mass[pl.ds(step * 256, 256), :], 256
        )
        dense = dense + dense_ref[:, at]
        before = moments_ref[:, at]
        for odd in range(2):
            here = slice(odd * LANES, (odd + 1) * LANES)
            part = fold_rows(total[odd * 32 : odd * 32 + 32, here], 8)
            sums_ref[pair * 2 + odd, 0:8, :] = part + before[:, here]
            sums_ref[pair * 2 + odd, 8:16, :] = dense[:, here]

    in_turn(blocks // 2, build, sums)
    total = sums_ref[:, 8, :]
    for row in range(9, 16):
        total = total + sums_ref[:, row, :]
    moments = [sums_ref[:, row, :] for row in range(8)]
    own = [fields_ref[:, row, :] - centre[row : row + 1, :] for row in range(8)]
    inverse = 1.0 / own[7]
    cube = inverse * inverse * inverse
    density = total * cube * (kernel_norm / 256.0)
    factor = cube * inverse * inverse * (20.0 * kernel_norm / 64.0)
    cross = own[0] * own[3] + own[1] * own[4] + own[2] * own[5]
    approach = cross * moments[6] + moments[7]
    for row in range(3):
        approach = approach - own[row + 3] * moments[row] - own[row] * moments[row + 3]
    press = entropy_ref[...] * inverse_cube_root(density)
    density_ref[...] = density
    divergence_ref[...] = factor * approach / density
    weight_ref[...] = (20.0 * kernel_norm) * own[6] * press * (cube * inverse * inverse)
    for row in range(3):
        gradient = (own[row] * moments[6] - moments[row]) * (factor * press)
        gradient_ref[row] = gradient


def inverse_cube_root(value):
    guess = jnp.exp(jnp.log(value) * (-1.0 / 3.0))
    guess = guess * (4.0 - value * guess * guess * guess) * (1.0 / 3.0)
    return guess * (4.0 - value * guess * guess * guess) * (1.0 / 3.0)


def prepare_second_kernel(fields_ref, centre_ref, weight_ref, near_ref, moment_ref, own_ref):
    blocks = fields_ref.shape[0]
    centre = centre_ref[...]

    @pl.loop(0, blocks // 4)
    def _(group):
        for part in range(4):
            index = group * 4 + part
            at = pl.ds(pl.multiple_of(index * LANES, LANES), LANES)
            near, moment_ref[:, at] = second_near(
                fields_ref[index], centre, weight_ref[pl.ds(index, 1), :]
            )
            near_ref[at, :] = near.T.astype(bf16)
            pos, _, square = particle_rows(fields_ref[index], centre)
            four = jnp.concatenate([pos * -2.0, square], axis=0)
            own_ref[:, at] = own_rows(four, [jnp.ones_like(square)] * 3)


def remote_second_kernel(
    capacity,
    extra,
    tables_ref,
    place_ref,
    me_ref,
    active_ref,
    slots_hbm,
    *refs,
):
    pieces, weight_pieces, refs = refs[:PIECES], refs[PIECES : PIECES + 4], refs[PIECES + 4 :]
    own_ref, fields_ref, centre_ref, moments_ref, gradient_ref, out_ref = refs[:6]
    gathered, weights, near0, near1, moment0, moment1 = refs[6:12]
    slots_ref, semaphore, weight_semaphore, slots_semaphore = refs[12:]
    blocks = fields_ref.shape[0]
    partners = slots_ref.shape[1]
    copies = fetch((slots_hbm,), slots_ref, slots_semaphore)
    copies += fetch(pieces, gathered, semaphore)
    copies += fetch(weight_pieces, weights, weight_semaphore)
    for copy in copies:
        copy.wait()
    centre = centre_ref[...]
    me = me_ref[0]
    sides = ((near0, moment0), (near1, moment1))

    def build(pair, side):
        near, moment = sides[side]
        for k in range(partners):
            at = slice(k * LANES, (k + 1) * LANES)
            rows = []
            for odd in range(2):
                row, weight_row = slot_place(
                    slots_ref[pair * 2 + odd, k],
                    tables_ref, place_ref, me, capacity, blocks, extra,
                )
                values, moments = second_near(
                    gathered[row], centre, weights[pl.ds(weight_row, 1), :]
                )
                rows.append(values)
                moment[odd * 16 : odd * 16 + 16, at] = moments
            near[at, :] = jnp.concatenate(rows, axis=0).T.astype(bf16)

    def sums(pair, side):
        near, moment = sides[side]
        at = pl.ds(pl.multiple_of(pair * 2 * LANES, 2 * LANES), 2 * LANES)
        _, total = pair_sums(diagonal(own_ref[:, at]), near, moment, None, 256)
        before = moments_ref[0:4, at]
        for odd in range(2):
            index = pair * 2 + odd
            here = slice(odd * LANES, (odd + 1) * LANES)
            part = fold_rows(total[odd * 16 : odd * 16 + 16, here], 4) + before[:, here]
            pos, _, _ = particle_rows(fields_ref[index], centre)
            out = gradient_ref[:, index, :] + (pos * part[3:4] - part[0:3])
            out_ref[index] = jnp.where(active_ref[index] > 0, out, 0.0)

    in_turn(blocks // 2, build, sums)


def join_kernel(*refs):
    count = (len(refs) - 1) // 3
    copies = []
    for number in range(count):
        out = refs[2 * count + number]
        start = 0
        for part in range(2):
            piece = refs[2 * number + part]
            copy = pltpu.make_async_copy(
                piece, out.at[pl.ds(start, piece.shape[0])], refs[-1].at[2 * number + part]
            )
            copy.start()
            copies.append(copy)
            start += piece.shape[0]
    for copy in copies:
        copy.wait()


def in_vmem(count):
    return [pl.BlockSpec(memory_space=pltpu.VMEM)] * count


def in_smem(count):
    return [pl.BlockSpec(memory_space=pltpu.SMEM)] * count


def in_any(count):
    return [pl.BlockSpec(memory_space=pl.ANY)] * count


def shape(*dims, dtype=f32):
    return jax.ShapeDtypeStruct(dims, dtype)


def room(mebibytes):
    return pltpu.CompilerParams(vmem_limit_bytes=mebibytes * 2**20)


def join(*pairs):
    flat = [item for pair in pairs for item in pair]
    outs = [shape(2 * pair[0].shape[0], *pair[0].shape[1:]) for pair in pairs]
    return pl.pallas_call(
        join_kernel,
        out_shape=outs,
        in_specs=in_any(len(flat)),
        out_specs=in_any(len(outs)),
        scratch_shapes=[pltpu.SemaphoreType.DMA((len(flat),))],
        compiler_params=room(4),
    )(*flat)


def assemble(extra, *arrays):
    blocks = arrays[0].shape[0]
    half = blocks // 2
    return pl.pallas_call(
        assemble_kernel,
        out_shape=[
            shape(blocks, 8, LANES),
            shape(half + extra, 8, LANES),
            shape(blocks - half, 8, LANES),
        ],
        in_specs=in_any(5),
        out_specs=in_vmem(3),
        scratch_shapes=[pltpu.VMEM(item.shape, item.dtype) for item in arrays]
        + [pltpu.SemaphoreType.DMA((5,))],
        compiler_params=room(8),
    )(*arrays)


def prepare(fields):
    particles = fields.shape[0] * LANES
    return pl.pallas_call(
        prepare_kernel,
        out_shape=[
            shape(particles, FEATS, dtype=bf16),
            shape(32, particles, dtype=bf16),
            shape(LANES, fields.shape[0]),
            shape(FEATS, particles, dtype=bf16),
            shape(8, LANES),
        ],
        in_specs=in_vmem(1),
        out_specs=in_vmem(5),
        compiler_params=room(16),
    )(fields)


def prepare_second(fields, centre, weight):
    particles = fields.shape[0] * LANES
    return pl.pallas_call(
        prepare_second_kernel,
        out_shape=[
            shape(particles, FEATS, dtype=bf16),
            shape(16, particles, dtype=bf16),
            shape(FEATS, particles, dtype=bf16),
        ],
        in_specs=in_vmem(3),
        out_specs=in_vmem(3),
        compiler_params=room(16),
    )(fields, centre, weight)


def local_pass(kernel, first, count, own, whole, sums):
    particles = own.shape[1]
    here = lambda index: (0, first + index)
    height = 2 if kernel is local_first_kernel else 1
    outs = [shape(8, particles)] * height
    aliases = {}
    operands = [own, *whole]
    in_specs = [pl.BlockSpec((FEATS, TILE), here)]
    in_specs += in_vmem(len(whole))
    if sums is not None:
        aliases = {len(operands) + number: number for number in range(height)}
        operands += list(sums)
        in_specs += in_any(height)
    return pl.pallas_call(
        kernel,
        grid=(count,),
        in_specs=in_specs,
        out_specs=[pl.BlockSpec((8, TILE), here)] * height,
        out_shape=outs,
        input_output_aliases=aliases,
        cost_estimate=pl.CostEstimate(
            flops=count * TILE * particles * 2000, bytes_accessed=2**20, transcendentals=0
        ),
        compiler_params=room(24),
    )(*operands)


def swap(value, bit, devices):
    return lax.ppermute(value, "dom", [(i, i ^ bit) for i in range(devices)])


def places(order, devices):
    table = np.zeros((devices,), np.int32)
    for apart in range(devices):
        table[apart] = sum(1 << k for k, bit in enumerate(order) if apart & bit)
    return table


def shares(tiles, stages):
    weights = [3] + [2] * (stages - 4) + [3, 5, 3]
    cuts = [round(tiles * sum(weights[:k]) / sum(weights)) for k in range(stages + 1)]
    return list(zip(cuts[:-1], cuts[1:]))


def per_device(
    devices,
    positions,
    velocities,
    masses,
    smoothing,
    entropy,
    export_blocks,
    partner_slots,
    active,
):
    blocks = positions.shape[0]
    particles = blocks * LANES
    capacity = export_blocks.shape[2]
    half = blocks // 2
    me = lax.axis_index("dom")
    extra = -(-devices * capacity // (8 * LANES))
    fields, first, second = assemble(
        extra, positions, velocities, masses, smoothing, export_blocks
    )
    bits = [1 << k for k in reversed(range(devices.bit_length() - 1))]
    order0 = list(bits)
    order1 = list(bits)
    order1[-3:-1] = reversed(order1[-3:-1])
    place = jnp.asarray(np.stack([places(order0, devices), places(order1, devices)]))
    tiles = particles // TILE
    stages = len(bits)

    near, moment, mass, own, centre = prepare(fields)
    sums = None
    first, second = [first], [second]
    for number, (start, stop) in enumerate(shares(tiles, stages)):
        first_in = [swap(item, order0[number], devices) for item in first]
        second_in = [swap(item, order1[number], devices) for item in second]
        if stop > start:
            sums = local_pass(
                local_first_kernel, start, stop - start, own, (near, moment, mass), sums
            )
        first += first_in
        second += second_in
        if number < stages - 1:
            first, second, near, sums = lax.optimization_barrier((first, second, near, sums))
        if number < stages - 2:
            first, second = join(first, second)
            first, second = [first], [second]
    pieces = (*first, *second)

    me_array = me.astype(jnp.int32).reshape(1)

    rows = sum(piece.shape[0] for piece in pieces)
    partners = partner_slots.shape[1] * LANES
    near_side = [pltpu.VMEM((partners, 2 * FEATS), bf16)] * 2
    density, divergence, weight, gradient, tables = pl.pallas_call(
        functools.partial(remote_first_kernel, capacity, extra),
        out_shape=[
            shape(blocks, LANES),
            shape(blocks, LANES),
            shape(blocks, LANES),
            shape(3, blocks, LANES),
            shape(devices, LANES, dtype=jnp.int32),
        ],
        in_specs=in_smem(2) + in_any(1 + PIECES) + in_vmem(6),
        out_specs=in_vmem(5),
        scratch_shapes=[
            pltpu.VMEM((rows, 8, LANES), f32),
            pltpu.SMEM((devices, LANES), jnp.int32),
            *near_side,
            pltpu.VMEM((64, partners), bf16),
            pltpu.VMEM((64, partners), bf16),
            pltpu.VMEM((partners, 2 * LANES), f32),
            pltpu.VMEM((partners, 2 * LANES), f32),
            pltpu.VMEM((blocks, 16, LANES), f32),
            pltpu.SMEM(partner_slots.shape, jnp.int32),
            pltpu.SemaphoreType.DMA((PIECES,)),
            pltpu.SemaphoreType.DMA,
            pltpu.SemaphoreType.DMA((1,)),
        ],
        compiler_params=room(20 + rows // 256),
    )(place, me_array, partner_slots, *pieces, own, fields, centre, entropy, *sums)

    near2, moment2, own2 = prepare_second(fields, centre, weight)
    sums = None
    weights = [weight]
    for number, (start, stop) in enumerate(shares(tiles, stages)):
        weights += [swap(item, order0[number], devices) for item in weights]
        if stop > start:
            sums = local_pass(
                local_second_kernel, start, stop - start, own2, (near2, moment2), sums
            )
        if number < stages - 1:
            weights, near2, sums = lax.optimization_barrier((weights, near2, sums))
        if number < stages - 2:
            weights = list(join(weights))

    acceleration = pl.pallas_call(
        functools.partial(remote_second_kernel, capacity, extra),
        out_shape=shape(blocks, 3, LANES),
        in_specs=in_smem(4) + in_any(5 + PIECES) + in_vmem(5),
        out_specs=pl.BlockSpec(memory_space=pltpu.VMEM),
        scratch_shapes=[
            pltpu.VMEM((rows, 8, LANES), f32),
            pltpu.VMEM((devices * blocks, LANES), f32),
            *near_side,
            pltpu.VMEM((32, partners), bf16),
            pltpu.VMEM((32, partners), bf16),
            pltpu.SMEM(partner_slots.shape, jnp.int32),
            pltpu.SemaphoreType.DMA((PIECES,)),
            pltpu.SemaphoreType.DMA((4,)),
            pltpu.SemaphoreType.DMA((1,)),
        ],
        compiler_params=room(20 + rows // 256),
    )(
        tables, place, me_array, active, partner_slots, *pieces, *weights, own2,
        fields, centre, *sums, gradient,
    )
    return (density, divergence, acceleration)


def solution(mesh):
    in_specs = (
        P("dom", None, None),
        P("dom", None, None),
        P("dom", None),
        P("dom", None),
        P("dom", None),
        P("dom", None, None),
        P("dom", None),
        P("dom"),
    )
    out_specs = (P("dom", None), P("dom", None), P("dom", None, None))
    return jax.shard_map(
        functools.partial(per_device, mesh.shape["dom"]),
        mesh=mesh,
        in_specs=in_specs,
        out_specs=out_specs,
        check_vma=False,
    )
```

```python
import functools

import jax
import jax.numpy as jnp
import numpy as np
from jax import lax
from jax.experimental import pallas as pl
from jax.experimental.pallas import tpu as pltpu
from jax.sharding import PartitionSpec as P

kernel_norm = 3.3422538049298023
LANES = 128
FEATS = 48
TILE = 256
PIECES = 8
bf16 = jnp.bfloat16
f32 = jnp.float32


def split3(value):
    high = value.astype(bf16).astype(f32)
    rest = value - high
    middle = rest.astype(bf16).astype(f32)
    return high, middle, rest - middle


def near_rows(four, fifth):
    high, middle, low = split3(jnp.concatenate([four, four], axis=0))
    upper = lax.broadcasted_iota(jnp.int32, high.shape, 0) < 4
    mixed = jnp.where(upper, high, middle)
    parts = split3(fifth)
    rows = [high, middle, low, mixed, *parts, *parts, *parts[:2], jnp.zeros((8, LANES), f32)]
    return jnp.concatenate(rows, axis=0).astype(bf16)


def own_rows(four, fifth):
    high, middle, low = split3(four)
    parts = split3(fifth)
    rows = [high, middle] * 3 + [low, low]
    rows += [parts[0]] * 3 + [parts[1]] * 3 + [parts[2]] * 2
    rows.append(jnp.zeros((8, LANES), f32))
    return jnp.concatenate(rows, axis=0).astype(bf16)


def fold_rows(moments, count):
    return moments[0:count] + (moments[count : 2 * count] + moments[2 * count : 3 * count])


def particle_rows(fields, centre):
    shifted = fields - centre
    pos = shifted[0:3]
    vel = shifted[3:6]
    square = jnp.sum(pos * pos, axis=0, keepdims=True)
    return pos, vel, square


def first_near(fields, centre):
    pos, vel, square = particle_rows(fields, centre)
    root = fields[6:7]
    scale = root * root
    cross = jnp.sum(pos * vel, axis=0, keepdims=True)
    near = near_rows(jnp.concatenate([pos * scale, scale], axis=0), square * scale)
    value = jnp.concatenate([pos, vel, jnp.ones_like(square), cross], axis=0) * root
    blank = jnp.zeros((5, LANES), f32)
    moments = jnp.concatenate([*split3(value), *split3(square * root), blank], axis=0)
    return near, moments.astype(bf16)


def second_near(fields, centre, weight):
    pos, _, square = particle_rows(fields, centre)
    scale = fields[7:8]
    near = near_rows(jnp.concatenate([pos * scale, scale], axis=0), square * scale)
    value = jnp.concatenate([pos * weight, weight], axis=0)
    moments = jnp.concatenate([*split3(value), jnp.zeros((4, LANES), f32)], axis=0)
    return near, moments.astype(bf16)


def spread(columns, number):
    return jnp.broadcast_to(columns[:, number : number + 1], (LANES, LANES))


def assemble_kernel(devices, capacity, stack_ref, fields_ref, first_ref, second_ref):
    blocks = fields_ref.shape[0]
    half = second_ref.shape[0]
    for row in range(6):
        fields_ref[:, row, :] = stack_ref[row]
    fields_ref[:, 6, :] = jnp.sqrt(jnp.sqrt(stack_ref[6]))
    smooth = stack_ref[7]
    fields_ref[:, 7, :] = 1.0 / (smooth * smooth)
    first_ref[0 : blocks - half] = fields_ref[0 : blocks - half]
    second_ref[...] = fields_ref[blocks - half :]
    each = LANES // capacity
    for number, start in enumerate(range(0, devices, 8 * each)):
        lines = [
            stack_ref[8 + row // blocks, row % blocks : row % blocks + 8, 0:capacity]
            for row in range(start, min(start + 8 * each, devices), 8)
        ]
        line = jnp.concatenate(lines, axis=1)
        first_ref[blocks - half + number, :, 0 : line.shape[1]] = line


def prepare_kernel(fields_ref, near_ref, moment_ref, root_ref, own_ref, centre_ref):
    blocks = fields_ref.shape[0]
    total = jnp.sum(fields_ref[...], axis=0)
    mean = jnp.sum(total, axis=1, keepdims=True) / (blocks * LANES)
    rows = lax.broadcasted_iota(jnp.int32, (8, LANES), 0)
    centre = jnp.where(rows < 6, jnp.broadcast_to(mean, (8, LANES)), 0.0)
    centre_ref[...] = centre
    root_ref[...] = fields_ref[:, 6, :].T

    @pl.loop(0, blocks // 4)
    def _(group):
        for part in range(4):
            index = group * 4 + part
            fields = fields_ref[index]
            at = pl.ds(pl.multiple_of(index * LANES, LANES), LANES)
            near, moment_ref[:, at] = first_near(fields, centre)
            near_ref[at, :] = near.T
            pos, _, square = particle_rows(fields, centre)
            scale = fields[7:8]
            four = jnp.concatenate([pos * (-2.0 * scale), square * scale], axis=0)
            own_ref[:, at] = own_rows(four, scale)


def halves(slope):
    high = slope.astype(bf16)
    low = (slope - high.astype(f32)).astype(bf16)
    return jnp.concatenate([high, low], axis=0)


def pair_sums(own, near_ref, moment_ref, root_of, chunk, beside=None):
    steps = near_ref.shape[0] // chunk
    dense = None
    total = None

    def place(step):
        return pl.ds(step * chunk, chunk)

    def product(step):
        return jnp.dot(near_ref[place(step), :], own, preferred_element_type=f32)

    def moment(step, slope):
        fields = moment_ref[:, place(step)]
        both = jnp.concatenate([fields, fields], axis=1)
        return jnp.dot(both, slope, preferred_element_type=f32)

    square = product(0)
    slope = None
    for step in range(steps):
        following = product(step + 1) if step + 1 < steps else None
        if beside is not None:
            beside(step, steps)
        square = jnp.maximum(square, 1e-12)
        radius = square * lax.rsqrt(square)
        if root_of is None:
            tail = jnp.maximum(1.0 - radius, 0.0)
            cube = tail * tail * tail
        else:
            tail = jnp.maximum(root_of(step) - radius, 0.0)
            cube = tail * tail * tail
            value = cube * radius
            value = jnp.sum(value.reshape(chunk // 8, 8, value.shape[1]), axis=0)
            dense = value if dense is None else dense + value
        if slope is not None:
            more = moment(step - 1, slope)
            total = more if total is None else total + more
        slope = halves(cube)
        square = following
    more = moment(steps - 1, slope)
    total = more if total is None else total + more
    return dense, total


def all_rows(dense, total):
    square = total[24:25] + (total[25:26] + total[26:27])
    last = [square, jnp.sum(dense, axis=0, keepdims=True), jnp.zeros((6, dense.shape[1]), f32)]
    return jnp.concatenate([fold_rows(total, 8), *last], axis=0)


def columns_of(columns, tiles):
    def root_of(step):
        rows = []
        for part in range(2):
            line = [spread(columns, tile(2 * step + part)) for tile in tiles]
            rows.append(jnp.concatenate(line, axis=1))
        return jnp.concatenate(rows, axis=0)

    return root_of


def local_first_kernel(own_ref, near_ref, moment_ref, root_ref, *refs):
    out_ref = refs[-1]
    own = own_ref[...]
    root_of = columns_of(root_ref[...], [lambda block: block] * (own.shape[1] // LANES))
    out_ref[...] = all_rows(*pair_sums(own, near_ref, moment_ref, root_of, 2 * LANES))


def local_second_kernel(own_ref, near_ref, moment_ref, *refs):
    out_ref = refs[-1]
    own = own_ref[...]
    _, total = pair_sums(own, near_ref, moment_ref, None, 2 * LANES)
    blank = jnp.zeros((4, own.shape[1]), f32)
    out_ref[...] = jnp.concatenate([fold_rows(total, 4), blank], axis=0)


def diagonal(own):
    blank = jnp.zeros((FEATS, LANES), bf16)
    upper = jnp.concatenate([own[:, 0:LANES], blank], axis=1)
    lower = jnp.concatenate([blank, own[:, LANES:]], axis=1)
    return jnp.concatenate([upper, lower], axis=0)


def slot_rows(slot, rows_ref, me, capacity):
    if capacity & (capacity - 1) == 0:
        sender = lax.shift_right_logical(slot, capacity.bit_length() - 1)
        within = slot & (capacity - 1)
    else:
        sender, within = lax.div(slot, capacity), lax.rem(slot, capacity)
    both = rows_ref[sender, me // 8 * capacity % LANES + within]
    return both & 0xFFFF, lax.shift_right_logical(both, 16)


def fetch(pieces, gathered, semaphore):
    start = 0
    copies = []
    for number, piece in enumerate(pieces):
        count = piece.shape[0]
        copy = pltpu.make_async_copy(
            piece, gathered.at[pl.ds(start, count)], semaphore.at[number]
        )
        copy.start()
        copies.append(copy)
        start += count
    return copies


def in_turn(pairs, partners, take, build, sums):
    def beside(pair, side):
        def part(step, steps):
            some = range(step * partners // steps, (step + 1) * partners // steps)
            taken = [take(pair, k) for k in some]
            for k, fields in zip(some, taken):
                build(fields, side, k)

        return part

    beside(0, 0)(0, 1)

    @pl.loop(0, pairs // 2 - 1)
    def _(step):
        sums(step * 2, 0, beside(step * 2 + 1, 1))
        sums(step * 2 + 1, 1, beside(step * 2 + 2, 0))

    sums(pairs - 2, 0, beside(pairs - 1, 1))
    sums(pairs - 1, 1, None)


def own_tables(gathered, line_ref, step, place_ref, me, capacity, blocks):
    half = blocks // 2
    line = me // 8 * capacity // LANES
    devices = line_ref.shape[0]
    chosen = lax.broadcasted_iota(jnp.int32, (8, LANES), 0) == me % 8
    for sender in range(devices):
        first = place_ref[0, sender ^ me]
        second = place_ref[1, sender ^ me]
        block = gathered[first * step + half + line]
        row = jnp.sum(jnp.where(chosen, block, 0.0), axis=0, keepdims=True).astype(jnp.int32)
        place = jnp.where(
            row < half, first * step + row, devices * step + second * half + row - half
        )
        line_ref[sender : sender + 1, :] = place + ((first * blocks + row) << 16)


def remote_first_kernel(capacity, extra, me_ref, *refs):
    pieces, (slots_hbm, place_hbm, entropy_hbm) = refs[:PIECES], refs[PIECES : PIECES + 3]
    refs = refs[PIECES + 3 :]
    own_ref, fields_ref, centre_ref, moments_ref = refs[:4]
    density_ref, divergence_ref, weight_ref, gradient_ref, line_ref, gathered = refs[4:10]
    tables_ref, near0, near1, moment0, moment1, root0, root1 = refs[10:17]
    sums_ref, slots_ref, place_ref, entropy_ref, semaphore, table_semaphore, small = refs[17:]
    blocks = fields_ref.shape[0]
    partners = slots_ref.shape[0]
    copies = fetch(pieces, gathered, semaphore)
    for number, (source, target) in enumerate(
        ((slots_hbm, slots_ref), (place_hbm, place_ref), (entropy_hbm, entropy_ref))
    ):
        copies += fetch((source,), target, small.at[pl.ds(number, 1)])
    for copy in copies:
        copy.wait()
    centre = centre_ref[...]
    me = me_ref[0]
    own_tables(gathered, line_ref, blocks // 2 + extra, place_ref, me, capacity, blocks)
    copy = pltpu.make_async_copy(line_ref, tables_ref, table_semaphore)
    copy.start()
    copy.wait()
    sides = ((near0, moment0, root0), (near1, moment1, root1))

    def take(pair, k):
        rows = [
            slot_rows(slots_ref[k, pair * 2 + odd], tables_ref, me, capacity)[0]
            for odd in range(2)
        ]
        return [gathered[row] for row in rows]

    def build(fields, side, k):
        near, moment, root = sides[side]
        at = slice(k * LANES, (k + 1) * LANES)
        rows = []
        for odd in range(2):
            values, moments = first_near(fields[odd], centre)
            rows.append(values)
            moment[odd * 32 : odd * 32 + 32, at] = moments
            line = odd * partners + k
            root[line : line + 1, :] = fields[odd][6:7]
        near[at, :] = jnp.concatenate(rows, axis=0).T

    def sums(pair, side, beside):
        near, moment, root = sides[side]
        at = pl.ds(pl.multiple_of(pair * 2 * LANES, 2 * LANES), 2 * LANES)
        root_of = columns_of(root[...].T, [lambda k: k, lambda k: partners + k])
        dense, total = pair_sums(
            diagonal(own_ref[:, at]), near, moment, root_of, 2 * LANES, beside
        )
        before = moments_ref[:, at]
        for odd in range(2):
            here = slice(odd * LANES, (odd + 1) * LANES)
            part = all_rows(dense[:, here], total[odd * 32 : odd * 32 + 32, here])
            sums_ref[pair * 2 + odd] = part + before[:, here]

    in_turn(blocks // 2, partners, take, build, sums)
    moments = [sums_ref[:, row, :] for row in range(10)]
    own = [fields_ref[:, row, :] - centre[row : row + 1, :] for row in range(8)]
    inverse_square = own[7]
    cube = inverse_square * jnp.sqrt(inverse_square)
    square = own[0] * own[0] + own[1] * own[1] + own[2] * own[2]
    cross = own[0] * own[3] + own[1] * own[4] + own[2] * own[5]
    shift = own[0] * moments[0] + own[1] * moments[1] + own[2] * moments[2]
    spread_out = (square * moments[6] + moments[8] - 2.0 * shift) * inverse_square
    density = kernel_norm * cube * (moments[6] + 3.0 * moments[9] - 4.0 * spread_out)
    factor = (20.0 * kernel_norm) * cube * inverse_square
    approach = cross * moments[6] + moments[7]
    for row in range(3):
        approach = approach - own[row + 3] * moments[row] - own[row] * moments[row + 3]
    press = entropy_ref[...] * inverse_cube_root(density)
    mass = own[6] * own[6]
    density_ref[...] = density
    divergence_ref[...] = factor * approach / density
    weight_ref[...] = factor * (mass * mass) * press
    for row in range(3):
        gradient = (own[row] * moments[6] - moments[row]) * (factor * press)
        gradient_ref[row] = gradient


def inverse_cube_root(value):
    guess = jnp.exp(jnp.log(value) * (-1.0 / 3.0))
    guess = guess * (4.0 - value * guess * guess * guess) * (1.0 / 3.0)
    return guess * (4.0 - value * guess * guess * guess) * (1.0 / 3.0)


def prepare_second_kernel(fields_ref, centre_ref, weight_ref, near_ref, moment_ref, own_ref):
    blocks = fields_ref.shape[0]
    centre = centre_ref[...]

    @pl.loop(0, blocks // 4)
    def _(group):
        for part in range(4):
            index = group * 4 + part
            at = pl.ds(pl.multiple_of(index * LANES, LANES), LANES)
            near, moment_ref[:, at] = second_near(
                fields_ref[index], centre, weight_ref[pl.ds(index, 1), :]
            )
            near_ref[at, :] = near.T
            pos, _, square = particle_rows(fields_ref[index], centre)
            four = jnp.concatenate([pos * -2.0, square], axis=0)
            own_ref[:, at] = own_rows(four, jnp.ones_like(square))


def remote_second_kernel(capacity, me_ref, *refs):
    pieces, (slots_hbm, tables_hbm, active_hbm) = refs[:4], refs[4:7]
    gathered, own_ref, fields_ref, centre_ref, moments_ref, gradient_ref, out_ref = refs[7:14]
    weights, near0, near1, moment0, moment1, slots_ref, tables_ref, active_ref = refs[14:22]
    semaphore, small = refs[22:]
    blocks = fields_ref.shape[0]
    partners = slots_ref.shape[0]
    copies = fetch(pieces, weights, semaphore)
    for number, (source, target) in enumerate(
        ((slots_hbm, slots_ref), (tables_hbm, tables_ref), (active_hbm, active_ref))
    ):
        copies += fetch((source,), target, small.at[pl.ds(number, 1)])
    for copy in copies:
        copy.wait()
    centre = centre_ref[...]
    me = me_ref[0]
    sides = ((near0, moment0), (near1, moment1))

    def take(pair, k):
        rows = [
            slot_rows(slots_ref[k, pair * 2 + odd], tables_ref, me, capacity) for odd in range(2)
        ]
        return [(gathered[row], weights[pl.ds(line, 1), :]) for row, line in rows]

    def build(fields, side, k):
        near, moment = sides[side]
        at = slice(k * LANES, (k + 1) * LANES)
        rows = []
        for odd in range(2):
            values, moments = second_near(fields[odd][0], centre, fields[odd][1])
            rows.append(values)
            moment[odd * 16 : odd * 16 + 16, at] = moments
        near[at, :] = jnp.concatenate(rows, axis=0).T

    def sums(pair, side, beside):
        near, moment = sides[side]
        at = pl.ds(pl.multiple_of(pair * 2 * LANES, 2 * LANES), 2 * LANES)
        _, total = pair_sums(diagonal(own_ref[:, at]), near, moment, None, 256, beside)
        before = moments_ref[0:4, at]
        for odd in range(2):
            index = pair * 2 + odd
            here = slice(odd * LANES, (odd + 1) * LANES)
            part = fold_rows(total[odd * 16 : odd * 16 + 16, here], 4) + before[:, here]
            pos, _, _ = particle_rows(fields_ref[index], centre)
            out = gradient_ref[:, index, :] + (pos * part[3:4] - part[0:3])
            out_ref[:, index, :] = jnp.where(active_ref[index] > 0, out, 0.0)

    in_turn(blocks // 2, partners, take, build, sums)


def join_kernel(*refs):
    count = (len(refs) - 1) // 3
    copies = []
    for number in range(count):
        out = refs[2 * count + number]
        start = 0
        for part in range(2):
            piece = refs[2 * number + part]
            copy = pltpu.make_async_copy(
                piece, out.at[pl.ds(start, piece.shape[0])], refs[-1].at[2 * number + part]
            )
            copy.start()
            copies.append(copy)
            start += piece.shape[0]
    for copy in copies:
        copy.wait()


def in_vmem(count):
    return [pl.BlockSpec(memory_space=pltpu.VMEM)] * count


def in_smem(count):
    return [pl.BlockSpec(memory_space=pltpu.SMEM)] * count


def in_any(count):
    return [pl.BlockSpec(memory_space=pl.ANY)] * count


def shape(*dims, dtype=f32):
    return jax.ShapeDtypeStruct(dims, dtype)


def room(mebibytes):
    return pltpu.CompilerParams(vmem_limit_bytes=mebibytes * 2**20)


def join(*pairs):
    flat = [item for pair in pairs for item in pair]
    outs = [shape(2 * pair[0].shape[0], *pair[0].shape[1:]) for pair in pairs]
    return pl.pallas_call(
        join_kernel,
        out_shape=outs,
        in_specs=in_any(len(flat)),
        out_specs=in_any(len(outs)),
        scratch_shapes=[pltpu.SemaphoreType.DMA((len(flat),))],
        compiler_params=room(4),
    )(*flat)


def assemble(extra, stack, devices, capacity):
    blocks = stack.shape[1]
    half = blocks // 2
    return pl.pallas_call(
        functools.partial(assemble_kernel, devices, capacity),
        out_shape=[
            shape(blocks, 8, LANES),
            shape(half + extra, 8, LANES),
            shape(blocks - half, 8, LANES),
        ],
        in_specs=in_vmem(1),
        out_specs=in_vmem(3),
        compiler_params=room(8),
    )(stack)


def prepare(fields):
    particles = fields.shape[0] * LANES
    return pl.pallas_call(
        prepare_kernel,
        out_shape=[
            shape(particles, FEATS, dtype=bf16),
            shape(32, particles, dtype=bf16),
            shape(LANES, fields.shape[0]),
            shape(FEATS, particles, dtype=bf16),
            shape(8, LANES),
        ],
        in_specs=in_vmem(1),
        out_specs=in_vmem(5),
        compiler_params=room(16),
    )(fields)


def prepare_second(fields, centre, weight):
    particles = fields.shape[0] * LANES
    return pl.pallas_call(
        prepare_second_kernel,
        out_shape=[
            shape(particles, FEATS, dtype=bf16),
            shape(16, particles, dtype=bf16),
            shape(FEATS, particles, dtype=bf16),
        ],
        in_specs=in_vmem(3),
        out_specs=in_vmem(3),
        compiler_params=room(16),
    )(fields, centre, weight)


def local_pass(kernel, first, count, own, whole, sums):
    particles = own.shape[1]
    here = lambda index: (0, first + index)
    height = 16 if kernel is local_first_kernel else 8
    aliases = {}
    operands = [own, *whole]
    in_specs = [pl.BlockSpec((FEATS, TILE), here)]
    in_specs += in_vmem(len(whole))
    if sums is not None:
        aliases = {len(operands): 0}
        operands.append(sums)
        in_specs += in_any(1)
    return pl.pallas_call(
        kernel,
        grid=(count,),
        in_specs=in_specs,
        out_specs=pl.BlockSpec((height, TILE), here),
        out_shape=shape(height, particles),
        input_output_aliases=aliases,
        cost_estimate=pl.CostEstimate(
            flops=count * TILE * particles * 2000, bytes_accessed=2**20, transcendentals=0
        ),
        compiler_params=room(24),
    )(*operands)


def swap(value, bit, devices):
    return lax.ppermute(value, "dom", [(i, i ^ bit) for i in range(devices)])


def places(order, devices):
    table = np.zeros((devices,), np.int32)
    for apart in range(devices):
        table[apart] = sum(1 << k for k, bit in enumerate(order) if apart & bit)
    return table


def shares(tiles, stages):
    weights = [3] + [2] * (stages - 4) + [3, 5, 3]
    cuts = [round(tiles * sum(weights[:k]) / sum(weights)) for k in range(stages + 1)]
    return list(zip(cuts[:-1], cuts[1:]))


def per_device(
    devices,
    positions,
    velocities,
    masses,
    smoothing,
    entropy,
    export_blocks,
    partner_slots,
    active,
):
    blocks = positions.shape[0]
    particles = blocks * LANES
    capacity = export_blocks.shape[2]
    half = blocks // 2
    me = lax.axis_index("dom")
    extra = -(-devices * capacity // (8 * LANES))
    table = export_blocks.reshape(devices // blocks, blocks, capacity)
    layers = [
        jnp.transpose(positions, (1, 0, 2)),
        jnp.transpose(velocities, (1, 0, 2)),
        masses[None],
        smoothing[None],
    ]
    height = 8 + table.shape[0]
    stack = jnp.pad(table, ((8, 0), (0, 0), (0, LANES - capacity))).astype(f32)
    start = 0
    for layer in layers:
        after = height - start - layer.shape[0]
        stack = stack + jnp.pad(layer, ((start, after), (0, 0), (0, 0)))
        start += layer.shape[0]
    fields, first, second = assemble(extra, stack, devices, capacity)
    bits = [1 << k for k in reversed(range(devices.bit_length() - 1))]
    order0 = list(bits)
    order1 = list(bits)
    order1[-3:-1] = reversed(order1[-3:-1])
    place = jnp.asarray(np.stack([places(order0, devices), places(order1, devices)]))
    tiles = particles // TILE
    stages = len(bits)

    near, moment, root, own, centre = prepare(fields)
    sums = None
    first, second = [first], [second]
    for number, (start, stop) in enumerate(shares(tiles, stages)):
        first_in = [swap(item, order0[number], devices) for item in first]
        second_in = [swap(item, order1[number], devices) for item in second]
        if stop > start:
            sums = local_pass(
                local_first_kernel, start, stop - start, own, (near, moment, root), sums
            )
        first += first_in
        second += second_in
        if number < stages - 1:
            first, second, near, sums = lax.optimization_barrier((first, second, near, sums))
        if number < stages - 2:
            first, second = join(first, second)
            first, second = [first], [second]
    pieces = (*first, *second)

    me_array = me.astype(jnp.int32).reshape(1)

    rows = sum(piece.shape[0] for piece in pieces)
    slots = jnp.transpose(partner_slots)
    partners = slots.shape[0] * LANES
    near_side = [pltpu.VMEM((partners, 2 * FEATS), bf16)] * 2
    density, divergence, weight, gradient, tables, gathered = pl.pallas_call(
        functools.partial(remote_first_kernel, capacity, extra),
        out_shape=[
            shape(blocks, LANES),
            shape(blocks, LANES),
            shape(blocks, LANES),
            shape(3, blocks, LANES),
            shape(devices, LANES, dtype=jnp.int32),
            shape(rows, 8, LANES),
        ],
        in_specs=in_smem(1) + in_any(PIECES + 3) + in_vmem(4),
        out_specs=in_vmem(6),
        scratch_shapes=[
            pltpu.SMEM((devices, LANES), jnp.int32),
            *near_side,
            pltpu.VMEM((64, partners), bf16),
            pltpu.VMEM((64, partners), bf16),
            pltpu.VMEM((partners // LANES * 2, LANES), f32),
            pltpu.VMEM((partners // LANES * 2, LANES), f32),
            pltpu.VMEM((blocks, 16, LANES), f32),
            pltpu.SMEM(slots.shape, jnp.int32),
            pltpu.SMEM(place.shape, jnp.int32),
            pltpu.VMEM(entropy.shape, f32),
            pltpu.SemaphoreType.DMA((PIECES,)),
            pltpu.SemaphoreType.DMA,
            pltpu.SemaphoreType.DMA((3,)),
        ],
        compiler_params=room(20 + rows // 256),
    )(me_array, *pieces, slots, place, entropy, own, fields, centre, sums)

    near2, moment2, own2 = prepare_second(fields, centre, weight)
    sums = None
    weights = [weight]
    for number, (start, stop) in enumerate(shares(tiles, stages)):
        weights += [swap(item, order0[number], devices) for item in weights]
        if stop > start:
            sums = local_pass(
                local_second_kernel, start, stop - start, own2, (near2, moment2), sums
            )
        if number < stages - 1:
            weights, near2, sums = lax.optimization_barrier((weights, near2, sums))
        if number < stages - 2:
            weights = list(join(weights))

    acceleration = pl.pallas_call(
        functools.partial(remote_second_kernel, capacity),
        out_shape=shape(3, blocks, LANES),
        in_specs=in_smem(1) + in_any(7) + in_vmem(6),
        out_specs=pl.BlockSpec(memory_space=pltpu.VMEM),
        scratch_shapes=[
            pltpu.VMEM((devices * blocks, LANES), f32),
            *near_side,
            pltpu.VMEM((32, partners), bf16),
            pltpu.VMEM((32, partners), bf16),
            pltpu.SMEM(slots.shape, jnp.int32),
            pltpu.SMEM(tables.shape, jnp.int32),
            pltpu.SMEM(active.shape, jnp.int32),
            pltpu.SemaphoreType.DMA((4,)),
            pltpu.SemaphoreType.DMA((3,)),
        ],
        compiler_params=room(20 + rows // 256),
    )(
        me_array, *weights, slots, tables, active, gathered, own2, fields, centre,
        sums, gradient,
    )
    return (density, divergence, jnp.transpose(acceleration, (1, 0, 2)))


def solution(mesh):
    in_specs = (
        P("dom", None, None),
        P("dom", None, None),
        P("dom", None),
        P("dom", None),
        P("dom", None),
        P("dom", None, None),
        P("dom", None),
        P("dom"),
    )
    out_specs = (P("dom", None), P("dom", None), P("dom", None, None))
    return jax.shard_map(
        functools.partial(per_device, mesh.shape["dom"]),
        mesh=mesh,
        in_specs=in_specs,
        out_specs=out_specs,
        check_vma=False,
    )
```

```python
import functools

import jax
import jax.numpy as jnp
import numpy as np
from jax import lax
from jax.experimental import pallas as pl
from jax.experimental.pallas import tpu as pltpu
from jax.sharding import PartitionSpec as P

kernel_norm = 3.3422538049298023
LANES = 128
FEATS = 48
TILE = 256
PIECES = 8
bf16 = jnp.bfloat16
f32 = jnp.float32


def split3(value):
    high = value.astype(bf16).astype(f32)
    rest = value - high
    middle = rest.astype(bf16).astype(f32)
    return high, middle, rest - middle


def near_rows(four, parts):
    high, middle, low = split3(jnp.concatenate([four, four], axis=0))
    upper = lax.broadcasted_iota(jnp.int32, high.shape, 0) < 4
    mixed = jnp.where(upper, high, middle)
    rows = [high, middle, low, mixed, *parts, *parts, *parts[:2], jnp.zeros((8, LANES), f32)]
    return jnp.concatenate(rows, axis=0).astype(bf16)


def own_rows(four, fifth):
    high, middle, low = split3(four)
    parts = split3(fifth)
    rows = [high, middle] * 3 + [low, low]
    rows += [parts[0]] * 3 + [parts[1]] * 3 + [parts[2]] * 2
    rows.append(jnp.zeros((8, LANES), f32))
    return jnp.concatenate(rows, axis=0).astype(bf16)


def fold_rows(moments, count):
    return moments[0:count] + (moments[count : 2 * count] + moments[2 * count : 3 * count])


def particle_rows(fields, centre):
    shifted = fields - centre
    pos = shifted[0:3]
    vel = shifted[3:6]
    square = jnp.sum(pos * pos, axis=0, keepdims=True)
    return pos, vel, square


def first_near(fields, centre):
    pos, vel, square = particle_rows(fields, centre)
    root = fields[6:7]
    scale = root * root
    cross = jnp.sum(pos * vel, axis=0, keepdims=True)
    squares = split3(jnp.concatenate([square * scale, square * root], axis=0))
    fifth, weighted = ([part[row : row + 1] for part in squares] for row in range(2))
    near = near_rows(jnp.concatenate([pos * scale, scale], axis=0), fifth)
    value = jnp.concatenate([pos, vel, jnp.ones_like(square), cross], axis=0) * root
    blank = jnp.zeros((5, LANES), f32)
    moments = jnp.concatenate([*split3(value), *weighted, blank], axis=0)
    return near, moments.astype(bf16)


def second_near(fields, centre, weight):
    pos, _, square = particle_rows(fields, centre)
    scale = fields[7:8]
    value = split3(jnp.concatenate([pos * weight, weight, square * scale], axis=0))
    fifth = [part[4:5] for part in value]
    near = near_rows(jnp.concatenate([pos * scale, scale], axis=0), fifth)
    value = [part[0:4] for part in value]
    moments = jnp.concatenate([*value, jnp.zeros((4, LANES), f32)], axis=0)
    return near, moments.astype(bf16)


def spread(columns, number):
    return jnp.broadcast_to(columns[:, number : number + 1], (LANES, LANES))


def assemble_kernel(devices, capacity, stack_ref, fields_ref, first_ref, second_ref):
    blocks = fields_ref.shape[0]
    half = second_ref.shape[0]
    for row in range(6):
        fields_ref[:, row, :] = stack_ref[row]
    fields_ref[:, 6, :] = jnp.sqrt(jnp.sqrt(stack_ref[6]))
    smooth = stack_ref[7]
    fields_ref[:, 7, :] = 1.0 / (smooth * smooth)
    first_ref[0 : blocks - half] = fields_ref[0 : blocks - half]
    second_ref[...] = fields_ref[blocks - half :]
    each = LANES // capacity
    for number, start in enumerate(range(0, devices, 8 * each)):
        lines = [
            stack_ref[8 + row // blocks, row % blocks : row % blocks + 8, 0:capacity]
            for row in range(start, min(start + 8 * each, devices), 8)
        ]
        line = jnp.concatenate(lines, axis=1)
        first_ref[blocks - half + number, :, 0 : line.shape[1]] = line


def prepare_kernel(fields_ref, near_ref, moment_ref, root_ref, own_ref, centre_ref):
    blocks = fields_ref.shape[0]
    total = jnp.sum(fields_ref[...], axis=0)
    mean = jnp.sum(total, axis=1, keepdims=True) / (blocks * LANES)
    rows = lax.broadcasted_iota(jnp.int32, (8, LANES), 0)
    centre = jnp.where(rows < 6, jnp.broadcast_to(mean, (8, LANES)), 0.0)
    centre_ref[...] = centre
    root_ref[...] = fields_ref[:, 6, :].T

    @pl.loop(0, blocks // 4)
    def _(group):
        for part in range(4):
            index = group * 4 + part
            fields = fields_ref[index]
            at = pl.ds(pl.multiple_of(index * LANES, LANES), LANES)
            near, moment_ref[:, at] = first_near(fields, centre)
            near_ref[at, :] = near.T
            pos, _, square = particle_rows(fields, centre)
            scale = fields[7:8]
            four = jnp.concatenate([pos * (-2.0 * scale), square * scale], axis=0)
            own_ref[:, at] = own_rows(four, scale)


def halves(slope):
    high = slope.astype(bf16)
    low = (slope - high.astype(f32)).astype(bf16)
    return jnp.concatenate([high, low], axis=0)


def pair_sums(own, near_ref, moment_ref, root_of, chunk, beside=None):
    steps = near_ref.shape[0] // chunk
    dense = None
    total = None

    def place(step):
        return pl.ds(step * chunk, chunk)

    def product(step):
        return jnp.dot(near_ref[place(step), :], own, preferred_element_type=f32)

    def moment(step, slope):
        fields = moment_ref[:, place(step)]
        both = jnp.concatenate([fields, fields], axis=1)
        return jnp.dot(both, slope, preferred_element_type=f32)

    square = product(0)
    slope = None
    for step in range(steps):
        following = product(step + 1) if step + 1 < steps else None
        if beside is not None:
            beside(step, steps)
        square = jnp.maximum(square, 1e-12)
        radius = square * lax.rsqrt(square)
        if root_of is None:
            tail = jnp.maximum(1.0 - radius, 0.0)
            cube = tail * tail * tail
        else:
            tail = jnp.maximum(root_of(step) - radius, 0.0)
            cube = tail * tail * tail
            value = cube * radius
            value = jnp.sum(value.reshape(chunk // 8, 8, value.shape[1]), axis=0)
            dense = value if dense is None else dense + value
        if slope is not None:
            more = moment(step - 1, slope)
            total = more if total is None else total + more
        slope = halves(cube)
        square = following
    more = moment(steps - 1, slope)
    total = more if total is None else total + more
    return dense, total


def all_rows(dense, total):
    square = total[24:25] + (total[25:26] + total[26:27])
    last = [square, jnp.sum(dense, axis=0, keepdims=True), jnp.zeros((6, dense.shape[1]), f32)]
    return jnp.concatenate([fold_rows(total, 8), *last], axis=0)


def columns_of(columns, tiles):
    def root_of(step):
        rows = []
        for part in range(2):
            line = [spread(columns, tile(2 * step + part)) for tile in tiles]
            rows.append(jnp.concatenate(line, axis=1))
        return jnp.concatenate(rows, axis=0)

    return root_of


def local_first_kernel(own_ref, near_ref, moment_ref, root_ref, *refs):
    out_ref = refs[-1]
    own = own_ref[...]
    root_of = columns_of(root_ref[...], [lambda block: block] * (own.shape[1] // LANES))
    out_ref[...] = all_rows(*pair_sums(own, near_ref, moment_ref, root_of, 2 * LANES))


def local_second_kernel(own_ref, near_ref, moment_ref, *refs):
    out_ref = refs[-1]
    own = own_ref[...]
    _, total = pair_sums(own, near_ref, moment_ref, None, 2 * LANES)
    blank = jnp.zeros((4, own.shape[1]), f32)
    out_ref[...] = jnp.concatenate([fold_rows(total, 4), blank], axis=0)


def diagonal(own):
    blank = jnp.zeros((FEATS, LANES), bf16)
    upper = jnp.concatenate([own[:, 0:LANES], blank], axis=1)
    lower = jnp.concatenate([blank, own[:, LANES:]], axis=1)
    return jnp.concatenate([upper, lower], axis=0)


def slot_rows(slot, rows_ref, me, capacity):
    if capacity & (capacity - 1) == 0:
        sender = lax.shift_right_logical(slot, capacity.bit_length() - 1)
        within = slot & (capacity - 1)
    else:
        sender, within = lax.div(slot, capacity), lax.rem(slot, capacity)
    both = rows_ref[sender, me // 8 * capacity % LANES + within]
    return both & 0xFFFF, lax.shift_right_logical(both, 16)


def fetch(pieces, gathered, semaphore):
    start = 0
    copies = []
    for number, piece in enumerate(pieces):
        count = piece.shape[0]
        copy = pltpu.make_async_copy(
            piece, gathered.at[pl.ds(start, count)], semaphore.at[number]
        )
        copy.start()
        copies.append(copy)
        start += count
    return copies


def in_turn(pairs, partners, take, build, sums):
    def beside(pair, side):
        def part(step, steps):
            some = range(step * partners // steps, (step + 1) * partners // steps)
            taken = [take(pair, k) for k in some]
            for k, fields in zip(some, taken):
                build(fields, side, k)

        return part

    beside(0, 0)(0, 1)

    @pl.loop(0, pairs // 2 - 1)
    def _(step):
        sums(step * 2, 0, beside(step * 2 + 1, 1))
        sums(step * 2 + 1, 1, beside(step * 2 + 2, 0))

    sums(pairs - 2, 0, beside(pairs - 1, 1))
    sums(pairs - 1, 1, None)


def own_tables(gathered, line_ref, step, place_ref, me, capacity, blocks):
    half = blocks // 2
    line = me // 8 * capacity // LANES
    devices = line_ref.shape[0]
    chosen = lax.broadcasted_iota(jnp.int32, (8, LANES), 0) == me % 8
    for sender in range(devices):
        first = place_ref[0, sender ^ me]
        second = place_ref[1, sender ^ me]
        block = gathered[first * step + half + line]
        row = jnp.sum(jnp.where(chosen, block, 0.0), axis=0, keepdims=True).astype(jnp.int32)
        place = jnp.where(
            row < half, first * step + row, devices * step + second * half + row - half
        )
        line_ref[sender : sender + 1, :] = place + ((first * blocks + row) << 16)


def remote_first_kernel(capacity, extra, me_ref, *refs):
    pieces, (slots_hbm, place_hbm, entropy_hbm) = refs[:PIECES], refs[PIECES : PIECES + 3]
    refs = refs[PIECES + 3 :]
    own_ref, fields_ref, centre_ref, moments_ref = refs[:4]
    density_ref, divergence_ref, weight_ref, gradient_ref, line_ref, gathered = refs[4:10]
    tables_ref, near0, near1, moment0, moment1, root0, root1 = refs[10:17]
    sums_ref, slots_ref, place_ref, entropy_ref, semaphore, table_semaphore, small = refs[17:]
    blocks = fields_ref.shape[0]
    partners = slots_ref.shape[0]
    copies = fetch(pieces, gathered, semaphore)
    for number, (source, target) in enumerate(
        ((slots_hbm, slots_ref), (place_hbm, place_ref), (entropy_hbm, entropy_ref))
    ):
        copies += fetch((source,), target, small.at[pl.ds(number, 1)])
    for copy in copies:
        copy.wait()
    centre = centre_ref[...]
    me = me_ref[0]
    own_tables(gathered, line_ref, blocks // 2 + extra, place_ref, me, capacity, blocks)
    copy = pltpu.make_async_copy(line_ref, tables_ref, table_semaphore)
    copy.start()
    copy.wait()
    sides = ((near0, moment0, root0), (near1, moment1, root1))

    def take(pair, k):
        rows = [
            slot_rows(slots_ref[k, pair * 2 + odd], tables_ref, me, capacity)[0]
            for odd in range(2)
        ]
        return [gathered[row] for row in rows]

    def build(fields, side, k):
        near, moment, root = sides[side]
        at = slice(k * LANES, (k + 1) * LANES)
        rows = []
        for odd in range(2):
            values, moments = first_near(fields[odd], centre)
            rows.append(values)
            moment[odd * 32 : odd * 32 + 32, at] = moments
            line = odd * partners + k
            root[line : line + 1, :] = fields[odd][6:7]
        near[at, :] = jnp.concatenate(rows, axis=0).T

    def sums(pair, side, beside):
        near, moment, root = sides[side]
        at = pl.ds(pl.multiple_of(pair * 2 * LANES, 2 * LANES), 2 * LANES)
        root_of = columns_of(root[...].T, [lambda k: k, lambda k: partners + k])
        dense, total = pair_sums(
            diagonal(own_ref[:, at]), near, moment, root_of, 2 * LANES, beside
        )
        before = moments_ref[:, at]
        for odd in range(2):
            here = slice(odd * LANES, (odd + 1) * LANES)
            part = all_rows(dense[:, here], total[odd * 32 : odd * 32 + 32, here])
            sums_ref[pair * 2 + odd] = part + before[:, here]

    in_turn(blocks // 2, partners, take, build, sums)
    moments = [sums_ref[:, row, :] for row in range(10)]
    own = [fields_ref[:, row, :] - centre[row : row + 1, :] for row in range(8)]
    inverse_square = own[7]
    cube = inverse_square * jnp.sqrt(inverse_square)
    square = own[0] * own[0] + own[1] * own[1] + own[2] * own[2]
    cross = own[0] * own[3] + own[1] * own[4] + own[2] * own[5]
    shift = own[0] * moments[0] + own[1] * moments[1] + own[2] * moments[2]
    spread_out = (square * moments[6] + moments[8] - 2.0 * shift) * inverse_square
    density = kernel_norm * cube * (moments[6] + 3.0 * moments[9] - 4.0 * spread_out)
    factor = (20.0 * kernel_norm) * cube * inverse_square
    approach = cross * moments[6] + moments[7]
    for row in range(3):
        approach = approach - own[row + 3] * moments[row] - own[row] * moments[row + 3]
    press = entropy_ref[...] * inverse_cube_root(density)
    mass = own[6] * own[6]
    density_ref[...] = density
    divergence_ref[...] = factor * approach / density
    weight_ref[...] = factor * (mass * mass) * press
    for row in range(3):
        gradient = (own[row] * moments[6] - moments[row]) * (factor * press)
        gradient_ref[row] = gradient


def inverse_cube_root(value):
    guess = jnp.exp(jnp.log(value) * (-1.0 / 3.0))
    guess = guess * (4.0 - value * guess * guess * guess) * (1.0 / 3.0)
    return guess * (4.0 - value * guess * guess * guess) * (1.0 / 3.0)


def prepare_second_kernel(fields_ref, centre_ref, weight_ref, near_ref, moment_ref, own_ref):
    blocks = fields_ref.shape[0]
    centre = centre_ref[...]

    @pl.loop(0, blocks // 4)
    def _(group):
        for part in range(4):
            index = group * 4 + part
            at = pl.ds(pl.multiple_of(index * LANES, LANES), LANES)
            near, moment_ref[:, at] = second_near(
                fields_ref[index], centre, weight_ref[pl.ds(index, 1), :]
            )
            near_ref[at, :] = near.T
            pos, _, square = particle_rows(fields_ref[index], centre)
            four = jnp.concatenate([pos * -2.0, square], axis=0)
            own_ref[:, at] = own_rows(four, jnp.ones_like(square))


def remote_second_kernel(capacity, me_ref, *refs):
    pieces, (slots_hbm, tables_hbm, active_hbm) = refs[:4], refs[4:7]
    gathered, own_ref, fields_ref, centre_ref, moments_ref, gradient_ref, out_ref = refs[7:14]
    weights, near0, near1, moment0, moment1, slots_ref, tables_ref, active_ref = refs[14:22]
    semaphore, small = refs[22:]
    blocks = fields_ref.shape[0]
    partners = slots_ref.shape[0]
    copies = fetch(pieces, weights, semaphore)
    for number, (source, target) in enumerate(
        ((slots_hbm, slots_ref), (tables_hbm, tables_ref), (active_hbm, active_ref))
    ):
        copies += fetch((source,), target, small.at[pl.ds(number, 1)])
    for copy in copies:
        copy.wait()
    centre = centre_ref[...]
    me = me_ref[0]
    sides = ((near0, moment0), (near1, moment1))

    def take(pair, k):
        rows = [
            slot_rows(slots_ref[k, pair * 2 + odd], tables_ref, me, capacity) for odd in range(2)
        ]
        return [(gathered[row], weights[pl.ds(line, 1), :]) for row, line in rows]

    def build(fields, side, k):
        near, moment = sides[side]
        at = slice(k * LANES, (k + 1) * LANES)
        rows = []
        for odd in range(2):
            values, moments = second_near(fields[odd][0], centre, fields[odd][1])
            rows.append(values)
            moment[odd * 16 : odd * 16 + 16, at] = moments
        near[at, :] = jnp.concatenate(rows, axis=0).T

    def sums(pair, side, beside):
        near, moment = sides[side]
        at = pl.ds(pl.multiple_of(pair * 2 * LANES, 2 * LANES), 2 * LANES)
        _, total = pair_sums(diagonal(own_ref[:, at]), near, moment, None, 256, beside)
        before = moments_ref[0:4, at]
        for odd in range(2):
            index = pair * 2 + odd
            here = slice(odd * LANES, (odd + 1) * LANES)
            part = fold_rows(total[odd * 16 : odd * 16 + 16, here], 4) + before[:, here]
            pos, _, _ = particle_rows(fields_ref[index], centre)
            out = gradient_ref[:, index, :] + (pos * part[3:4] - part[0:3])
            out_ref[:, index, :] = jnp.where(active_ref[index] > 0, out, 0.0)

    in_turn(blocks // 2, partners, take, build, sums)


def join_kernel(*refs):
    count = (len(refs) - 1) // 3
    copies = []
    for number in range(count):
        out = refs[2 * count + number]
        start = 0
        for part in range(2):
            piece = refs[2 * number + part]
            copy = pltpu.make_async_copy(
                piece, out.at[pl.ds(start, piece.shape[0])], refs[-1].at[2 * number + part]
            )
            copy.start()
            copies.append(copy)
            start += piece.shape[0]
    for copy in copies:
        copy.wait()


def in_vmem(count):
    return [pl.BlockSpec(memory_space=pltpu.VMEM)] * count


def in_smem(count):
    return [pl.BlockSpec(memory_space=pltpu.SMEM)] * count


def in_any(count):
    return [pl.BlockSpec(memory_space=pl.ANY)] * count


def shape(*dims, dtype=f32):
    return jax.ShapeDtypeStruct(dims, dtype)


def room(mebibytes):
    return pltpu.CompilerParams(vmem_limit_bytes=mebibytes * 2**20)


def join(*pairs):
    flat = [item for pair in pairs for item in pair]
    outs = [shape(2 * pair[0].shape[0], *pair[0].shape[1:]) for pair in pairs]
    return pl.pallas_call(
        join_kernel,
        out_shape=outs,
        in_specs=in_any(len(flat)),
        out_specs=in_any(len(outs)),
        scratch_shapes=[pltpu.SemaphoreType.DMA((len(flat),))],
        compiler_params=room(4),
    )(*flat)


def assemble(extra, stack, devices, capacity):
    blocks = stack.shape[1]
    half = blocks // 2
    return pl.pallas_call(
        functools.partial(assemble_kernel, devices, capacity),
        out_shape=[
            shape(blocks, 8, LANES),
            shape(half + extra, 8, LANES),
            shape(blocks - half, 8, LANES),
        ],
        in_specs=in_vmem(1),
        out_specs=in_vmem(3),
        compiler_params=room(8),
    )(stack)


def prepare(fields):
    particles = fields.shape[0] * LANES
    return pl.pallas_call(
        prepare_kernel,
        out_shape=[
            shape(particles, FEATS, dtype=bf16),
            shape(32, particles, dtype=bf16),
            shape(LANES, fields.shape[0]),
            shape(FEATS, particles, dtype=bf16),
            shape(8, LANES),
        ],
        in_specs=in_vmem(1),
        out_specs=in_vmem(5),
        compiler_params=room(16),
    )(fields)


def prepare_second(fields, centre, weight):
    particles = fields.shape[0] * LANES
    return pl.pallas_call(
        prepare_second_kernel,
        out_shape=[
            shape(particles, FEATS, dtype=bf16),
            shape(16, particles, dtype=bf16),
            shape(FEATS, particles, dtype=bf16),
        ],
        in_specs=in_vmem(3),
        out_specs=in_vmem(3),
        compiler_params=room(16),
    )(fields, centre, weight)


def local_pass(kernel, first, count, own, whole, sums):
    particles = own.shape[1]
    here = lambda index: (0, first + index)
    height = 16 if kernel is local_first_kernel else 8
    aliases = {}
    operands = [own, *whole]
    in_specs = [pl.BlockSpec((FEATS, TILE), here)]
    in_specs += in_vmem(len(whole))
    if sums is not None:
        aliases = {len(operands): 0}
        operands.append(sums)
        in_specs += in_any(1)
    return pl.pallas_call(
        kernel,
        grid=(count,),
        in_specs=in_specs,
        out_specs=pl.BlockSpec((height, TILE), here),
        out_shape=shape(height, particles),
        input_output_aliases=aliases,
        cost_estimate=pl.CostEstimate(
            flops=3 * TILE * particles * 2000, bytes_accessed=2**20, transcendentals=0
        ),
        compiler_params=room(24),
    )(*operands)


def swap(value, bit, devices):
    return lax.ppermute(value, "dom", [(i, i ^ bit) for i in range(devices)])


def places(order, devices):
    table = np.zeros((devices,), np.int32)
    for apart in range(devices):
        table[apart] = sum(1 << k for k, bit in enumerate(order) if apart & bit)
    return table


def shares(tiles, stages):
    weights = [3] * (stages - 2) + [5, 2]
    cuts = [round(tiles * sum(weights[:k]) / sum(weights)) for k in range(stages + 1)]
    return list(zip(cuts[:-1], cuts[1:]))


def per_device(
    devices,
    positions,
    velocities,
    masses,
    smoothing,
    entropy,
    export_blocks,
    partner_slots,
    active,
):
    blocks = positions.shape[0]
    particles = blocks * LANES
    capacity = export_blocks.shape[2]
    half = blocks // 2
    me = lax.axis_index("dom")
    extra = -(-devices * capacity // (8 * LANES))
    table = export_blocks.reshape(devices // blocks, blocks, capacity)
    layers = [
        jnp.transpose(positions, (1, 0, 2)),
        jnp.transpose(velocities, (1, 0, 2)),
        masses[None],
        smoothing[None],
    ]
    height = 8 + table.shape[0]
    stack = jnp.pad(table, ((8, 0), (0, 0), (0, LANES - capacity))).astype(f32)
    start = 0
    for layer in layers:
        after = height - start - layer.shape[0]
        stack = stack + jnp.pad(layer, ((start, after), (0, 0), (0, 0)))
        start += layer.shape[0]
    fields, first, second = assemble(extra, stack, devices, capacity)
    bits = [1 << k for k in reversed(range(devices.bit_length() - 1))]
    order0 = list(bits)
    order1 = list(bits)
    order1[-3:-1] = reversed(order1[-3:-1])
    place = jnp.asarray(np.stack([places(order0, devices), places(order1, devices)]))
    tiles = particles // TILE
    stages = len(bits)

    near, moment, root, own, centre = prepare(fields)
    sums = None
    first, second = [first], [second]
    for number, (start, stop) in enumerate(shares(tiles, stages)):
        first_in = [swap(item, order0[number], devices) for item in first]
        second_in = [swap(item, order1[number], devices) for item in second]
        if stop > start:
            sums = local_pass(
                local_first_kernel, start, stop - start, own, (near, moment, root), sums
            )
        first += first_in
        second += second_in
        if number < stages - 1:
            first, second, near, sums = lax.optimization_barrier((first, second, near, sums))
        if number < stages - 2:
            first, second = join(first, second)
            first, second = [first], [second]
    pieces = (*first, *second)

    me_array = me.astype(jnp.int32).reshape(1)

    rows = sum(piece.shape[0] for piece in pieces)
    slots = jnp.transpose(partner_slots)
    partners = slots.shape[0] * LANES
    near_side = [pltpu.VMEM((partners, 2 * FEATS), bf16)] * 2
    density, divergence, weight, gradient, tables, gathered = pl.pallas_call(
        functools.partial(remote_first_kernel, capacity, extra),
        out_shape=[
            shape(blocks, LANES),
            shape(blocks, LANES),
            shape(blocks, LANES),
            shape(3, blocks, LANES),
            shape(devices, LANES, dtype=jnp.int32),
            shape(rows, 8, LANES),
        ],
        in_specs=in_smem(1) + in_any(PIECES + 3) + in_vmem(4),
        out_specs=in_vmem(6),
        scratch_shapes=[
            pltpu.SMEM((devices, LANES), jnp.int32),
            *near_side,
            pltpu.VMEM((64, partners), bf16),
            pltpu.VMEM((64, partners), bf16),
            pltpu.VMEM((partners // LANES * 2, LANES), f32),
            pltpu.VMEM((partners // LANES * 2, LANES), f32),
            pltpu.VMEM((blocks, 16, LANES), f32),
            pltpu.SMEM(slots.shape, jnp.int32),
            pltpu.SMEM(place.shape, jnp.int32),
            pltpu.VMEM(entropy.shape, f32),
            pltpu.SemaphoreType.DMA((PIECES,)),
            pltpu.SemaphoreType.DMA,
            pltpu.SemaphoreType.DMA((3,)),
        ],
        compiler_params=room(20 + rows // 256),
    )(me_array, *pieces, slots, place, entropy, own, fields, centre, sums)

    near2, moment2, own2 = prepare_second(fields, centre, weight)
    sums = None
    weights = [weight]
    for number, (start, stop) in enumerate(shares(tiles, stages)):
        weights += [swap(item, order0[number], devices) for item in weights]
        if stop > start:
            sums = local_pass(
                local_second_kernel, start, stop - start, own2, (near2, moment2), sums
            )
        if number < stages - 1:
            weights, near2, sums = lax.optimization_barrier((weights, near2, sums))
        if number < stages - 2:
            weights = list(join(weights))

    acceleration = pl.pallas_call(
        functools.partial(remote_second_kernel, capacity),
        out_shape=shape(3, blocks, LANES),
        in_specs=in_smem(1) + in_any(7) + in_vmem(6),
        out_specs=pl.BlockSpec(memory_space=pltpu.VMEM),
        scratch_shapes=[
            pltpu.VMEM((devices * blocks, LANES), f32),
            *near_side,
            pltpu.VMEM((32, partners), bf16),
            pltpu.VMEM((32, partners), bf16),
            pltpu.SMEM(slots.shape, jnp.int32),
            pltpu.SMEM(tables.shape, jnp.int32),
            pltpu.SMEM(active.shape, jnp.int32),
            pltpu.SemaphoreType.DMA((4,)),
            pltpu.SemaphoreType.DMA((3,)),
        ],
        compiler_params=room(20 + rows // 256),
    )(
        me_array, *weights, slots, tables, active, gathered, own2, fields, centre,
        sums, gradient,
    )
    return (density, divergence, jnp.transpose(acceleration, (1, 0, 2)))


def solution(mesh):
    in_specs = (
        P("dom", None, None),
        P("dom", None, None),
        P("dom", None),
        P("dom", None),
        P("dom", None),
        P("dom", None, None),
        P("dom", None),
        P("dom"),
    )
    out_specs = (P("dom", None), P("dom", None), P("dom", None, None))
    return jax.shard_map(
        functools.partial(per_device, mesh.shape["dom"]),
        mesh=mesh,
        in_specs=in_specs,
        out_specs=out_specs,
        check_vma=False,
    )
```

```python
import functools

import jax
import jax.numpy as jnp
import numpy as np
from jax import lax
from jax.experimental import pallas as pl
from jax.experimental.pallas import tpu as pltpu
from jax.sharding import PartitionSpec as P

kernel_norm = 3.3422538049298023
LANES = 128
FEATS = 48
TILE = 256
PIECES = 8
bf16 = jnp.bfloat16
f32 = jnp.float32


def split3(value):
    high = value.astype(bf16).astype(f32)
    rest = value - high
    middle = rest.astype(bf16).astype(f32)
    return high, middle, rest - middle


def near_rows(four, parts):
    high, middle, low = split3(jnp.concatenate([four, four], axis=0))
    upper = lax.broadcasted_iota(jnp.int32, high.shape, 0) < 4
    mixed = jnp.where(upper, high, middle)
    rows = [high, middle, low, mixed, *parts, *parts, *parts[:2], jnp.zeros((8, LANES), f32)]
    return jnp.concatenate(rows, axis=0).astype(bf16)


def own_rows(four, fifth):
    high, middle, low = split3(four)
    parts = split3(fifth)
    rows = [high, middle] * 3 + [low, low]
    rows += [parts[0]] * 3 + [parts[1]] * 3 + [parts[2]] * 2
    rows.append(jnp.zeros((8, LANES), f32))
    return jnp.concatenate(rows, axis=0).astype(bf16)


def fold_rows(moments, count):
    return moments[0:count] + (moments[count : 2 * count] + moments[2 * count : 3 * count])


def particle_rows(fields, centre):
    shifted = fields - centre
    pos = shifted[0:3]
    vel = shifted[3:6]
    square = jnp.sum(pos * pos, axis=0, keepdims=True)
    return pos, vel, square


def first_near(fields, centre):
    pos, vel, square = particle_rows(fields, centre)
    root = fields[6:7]
    scale = root * root
    cross = jnp.sum(pos * vel, axis=0, keepdims=True)
    squares = split3(jnp.concatenate([square * scale, square * root], axis=0))
    fifth, weighted = ([part[row : row + 1] for part in squares] for row in range(2))
    near = near_rows(jnp.concatenate([pos * scale, scale], axis=0), fifth)
    value = jnp.concatenate([pos, vel, jnp.ones_like(square), cross], axis=0) * root
    blank = jnp.zeros((5, LANES), f32)
    moments = jnp.concatenate([*split3(value), *weighted, blank], axis=0)
    return near, moments.astype(bf16)


def second_near(fields, centre, weight):
    pos, _, square = particle_rows(fields, centre)
    scale = fields[7:8]
    value = split3(jnp.concatenate([pos * weight, weight, square * scale], axis=0))
    fifth = [part[4:5] for part in value]
    near = near_rows(jnp.concatenate([pos * scale, scale], axis=0), fifth)
    value = [part[0:4] for part in value]
    moments = jnp.concatenate([*value, jnp.zeros((4, LANES), f32)], axis=0)
    return near, moments.astype(bf16)


def spread(columns, number):
    return jnp.broadcast_to(columns[:, number : number + 1], (LANES, LANES))


def assemble_kernel(devices, capacity, stack_ref, fields_ref, payload_ref):
    blocks = fields_ref.shape[0]
    for row in range(6):
        fields_ref[:, row, :] = stack_ref[row]
    fields_ref[:, 6, :] = jnp.sqrt(jnp.sqrt(stack_ref[6]))
    smooth = stack_ref[7]
    fields_ref[:, 7, :] = 1.0 / (smooth * smooth)
    payload_ref[0:blocks] = fields_ref[...]
    each = LANES // capacity
    for number, start in enumerate(range(0, devices, 8 * each)):
        lines = [
            stack_ref[8 + row // blocks, row % blocks : row % blocks + 8, 0:capacity]
            for row in range(start, min(start + 8 * each, devices), 8)
        ]
        line = jnp.concatenate(lines, axis=1)
        payload_ref[blocks + number, :, 0 : line.shape[1]] = line


def prepare_kernel(fields_ref, near_ref, moment_ref, root_ref, own_ref, centre_ref):
    blocks = fields_ref.shape[0]
    total = jnp.sum(fields_ref[...], axis=0)
    mean = jnp.sum(total, axis=1, keepdims=True) / (blocks * LANES)
    rows = lax.broadcasted_iota(jnp.int32, (8, LANES), 0)
    centre = jnp.where(rows < 6, jnp.broadcast_to(mean, (8, LANES)), 0.0)
    centre_ref[...] = centre
    root_ref[...] = fields_ref[:, 6, :].T

    @pl.loop(0, blocks // 4)
    def _(group):
        for part in range(4):
            index = group * 4 + part
            fields = fields_ref[index]
            at = pl.ds(pl.multiple_of(index * LANES, LANES), LANES)
            near, moment_ref[:, at] = first_near(fields, centre)
            near_ref[at, :] = near.T
            pos, _, square = particle_rows(fields, centre)
            scale = fields[7:8]
            four = jnp.concatenate([pos * (-2.0 * scale), square * scale], axis=0)
            own_ref[:, at] = own_rows(four, scale)


def halves(slope):
    high = slope.astype(bf16)
    low = (slope - high.astype(f32)).astype(bf16)
    return jnp.concatenate([high, low], axis=0)


def pair_sums(own, near_ref, moment_ref, root_of, chunk, beside=None):
    steps = near_ref.shape[0] // chunk
    dense = None
    total = None

    def place(step):
        return pl.ds(step * chunk, chunk)

    def product(step):
        return jnp.dot(near_ref[place(step), :], own, preferred_element_type=f32)

    def moment(step, slope):
        fields = moment_ref[:, place(step)]
        both = jnp.concatenate([fields, fields], axis=1)
        return jnp.dot(both, slope, preferred_element_type=f32)

    square = product(0)
    slope = None
    for step in range(steps):
        following = product(step + 1) if step + 1 < steps else None
        if beside is not None:
            beside(step, steps)
        square = jnp.maximum(square, 1e-12)
        radius = square * lax.rsqrt(square)
        if root_of is None:
            tail = jnp.maximum(1.0 - radius, 0.0)
            cube = tail * tail * tail
        else:
            tail = jnp.maximum(root_of(step) - radius, 0.0)
            cube = tail * tail * tail
            value = cube * radius
            value = jnp.sum(value.reshape(chunk // 8, 8, value.shape[1]), axis=0)
            dense = value if dense is None else dense + value
        if slope is not None:
            more = moment(step - 1, slope)
            total = more if total is None else total + more
        slope = halves(cube)
        square = following
    more = moment(steps - 1, slope)
    total = more if total is None else total + more
    return dense, total


def all_rows(dense, total):
    square = total[24:25] + (total[25:26] + total[26:27])
    last = [square, jnp.sum(dense, axis=0, keepdims=True), jnp.zeros((6, dense.shape[1]), f32)]
    return jnp.concatenate([fold_rows(total, 8), *last], axis=0)


def columns_of(columns, tiles):
    def root_of(step):
        rows = []
        for part in range(2):
            line = [spread(columns, tile(2 * step + part)) for tile in tiles]
            rows.append(jnp.concatenate(line, axis=1))
        return jnp.concatenate(rows, axis=0)

    return root_of


def local_first_kernel(own_ref, near_ref, moment_ref, root_ref, *refs):
    out_ref = refs[-1]
    own = own_ref[...]
    root_of = columns_of(root_ref[...], [lambda block: block] * (own.shape[1] // LANES))
    out_ref[...] = all_rows(*pair_sums(own, near_ref, moment_ref, root_of, 2 * LANES))


def local_second_kernel(own_ref, near_ref, moment_ref, *refs):
    out_ref = refs[-1]
    own = own_ref[...]
    _, total = pair_sums(own, near_ref, moment_ref, None, 2 * LANES)
    blank = jnp.zeros((4, own.shape[1]), f32)
    out_ref[...] = jnp.concatenate([fold_rows(total, 4), blank], axis=0)


def diagonal(own):
    blank = jnp.zeros((FEATS, LANES), bf16)
    upper = jnp.concatenate([own[:, 0:LANES], blank], axis=1)
    lower = jnp.concatenate([blank, own[:, LANES:]], axis=1)
    return jnp.concatenate([upper, lower], axis=0)


def slot_rows(slot, rows_ref, me, capacity):
    if capacity & (capacity - 1) == 0:
        sender = lax.shift_right_logical(slot, capacity.bit_length() - 1)
        within = slot & (capacity - 1)
    else:
        sender, within = lax.div(slot, capacity), lax.rem(slot, capacity)
    both = rows_ref[sender, me // 8 * capacity % LANES + within]
    return both & 0xFFFF, lax.shift_right_logical(both, 16)


def fetch(pieces, gathered, semaphore):
    start = 0
    copies = []
    for number, piece in enumerate(pieces):
        count = piece.shape[0]
        copy = pltpu.make_async_copy(
            piece, gathered.at[pl.ds(start, count)], semaphore.at[number]
        )
        copy.start()
        copies.append(copy)
        start += count
    return copies


def in_turn(pairs, partners, take, build, sums):
    def beside(pair, side):
        def part(step, steps):
            some = range(step * partners // steps, (step + 1) * partners // steps)
            taken = [take(pair, k) for k in some]
            for k, fields in zip(some, taken):
                build(fields, side, k)

        return part

    beside(0, 0)(0, 1)

    @pl.loop(0, pairs // 2 - 1)
    def _(step):
        sums(step * 2, 0, beside(step * 2 + 1, 1))
        sums(step * 2 + 1, 1, beside(step * 2 + 2, 0))

    sums(pairs - 2, 0, beside(pairs - 1, 1))
    sums(pairs - 1, 1, None)


def own_tables(gathered, line_ref, step, place_ref, me, capacity, blocks):
    line = me // 8 * capacity // LANES
    devices = line_ref.shape[0]
    chosen = lax.broadcasted_iota(jnp.int32, (8, LANES), 0) == me % 8
    for sender in range(devices):
        first = place_ref[0, sender ^ me]
        second = place_ref[1, sender ^ me]
        block = gathered[first * step + blocks + line]
        row = jnp.sum(jnp.where(chosen, block, 0.0), axis=0, keepdims=True).astype(jnp.int32)
        line_ref[sender : sender + 1, :] = (
            first * step + row + ((second * blocks + row) << 16)
        )


def remote_first_kernel(capacity, extra, me_ref, *refs):
    pieces, (slots_hbm, place_hbm, entropy_hbm) = refs[:PIECES], refs[PIECES : PIECES + 3]
    refs = refs[PIECES + 3 :]
    own_ref, fields_ref, centre_ref, moments_ref = refs[:4]
    density_ref, divergence_ref, weight_ref, gradient_ref, line_ref, gathered = refs[4:10]
    tables_ref, near0, near1, moment0, moment1, root0, root1 = refs[10:17]
    sums_ref, slots_ref, place_ref, entropy_ref, semaphore, table_semaphore, small = refs[17:]
    blocks = fields_ref.shape[0]
    partners = slots_ref.shape[0]
    copies = fetch(pieces, gathered, semaphore)
    for number, (source, target) in enumerate(
        ((slots_hbm, slots_ref), (place_hbm, place_ref), (entropy_hbm, entropy_ref))
    ):
        copies += fetch((source,), target, small.at[pl.ds(number, 1)])
    for copy in copies:
        copy.wait()
    centre = centre_ref[...]
    me = me_ref[0]
    own_tables(gathered, line_ref, blocks + extra, place_ref, me, capacity, blocks)
    copy = pltpu.make_async_copy(line_ref, tables_ref, table_semaphore)
    copy.start()
    copy.wait()
    sides = ((near0, moment0, root0), (near1, moment1, root1))

    def take(pair, k):
        rows = [
            slot_rows(slots_ref[k, pair * 2 + odd], tables_ref, me, capacity)[0]
            for odd in range(2)
        ]
        return [gathered[row] for row in rows]

    def build(fields, side, k):
        near, moment, root = sides[side]
        at = slice(k * LANES, (k + 1) * LANES)
        rows = []
        for odd in range(2):
            values, moments = first_near(fields[odd], centre)
            rows.append(values)
            moment[odd * 32 : odd * 32 + 32, at] = moments
            line = odd * partners + k
            root[line : line + 1, :] = fields[odd][6:7]
        near[at, :] = jnp.concatenate(rows, axis=0).T

    def sums(pair, side, beside):
        near, moment, root = sides[side]
        at = pl.ds(pl.multiple_of(pair * 2 * LANES, 2 * LANES), 2 * LANES)
        root_of = columns_of(root[...].T, [lambda k: k, lambda k: partners + k])
        dense, total = pair_sums(
            diagonal(own_ref[:, at]), near, moment, root_of, 2 * LANES, beside
        )
        before = moments_ref[:, at]
        for odd in range(2):
            here = slice(odd * LANES, (odd + 1) * LANES)
            part = all_rows(dense[:, here], total[odd * 32 : odd * 32 + 32, here])
            sums_ref[pair * 2 + odd] = part + before[:, here]

    in_turn(blocks // 2, partners, take, build, sums)
    moments = [sums_ref[:, row, :] for row in range(10)]
    own = [fields_ref[:, row, :] - centre[row : row + 1, :] for row in range(8)]
    inverse_square = own[7]
    cube = inverse_square * jnp.sqrt(inverse_square)
    square = own[0] * own[0] + own[1] * own[1] + own[2] * own[2]
    cross = own[0] * own[3] + own[1] * own[4] + own[2] * own[5]
    shift = own[0] * moments[0] + own[1] * moments[1] + own[2] * moments[2]
    spread_out = (square * moments[6] + moments[8] - 2.0 * shift) * inverse_square
    density = kernel_norm * cube * (moments[6] + 3.0 * moments[9] - 4.0 * spread_out)
    factor = (20.0 * kernel_norm) * cube * inverse_square
    approach = cross * moments[6] + moments[7]
    for row in range(3):
        approach = approach - own[row + 3] * moments[row] - own[row] * moments[row + 3]
    press = entropy_ref[...] * inverse_cube_root(density)
    mass = own[6] * own[6]
    density_ref[...] = density
    divergence_ref[...] = factor * approach / density
    weight_ref[...] = factor * (mass * mass) * press
    for row in range(3):
        gradient = (own[row] * moments[6] - moments[row]) * (factor * press)
        gradient_ref[row] = gradient


def inverse_cube_root(value):
    guess = jnp.exp(jnp.log(value) * (-1.0 / 3.0))
    guess = guess * (4.0 - value * guess * guess * guess) * (1.0 / 3.0)
    return guess * (4.0 - value * guess * guess * guess) * (1.0 / 3.0)


def prepare_second_kernel(fields_ref, centre_ref, weight_ref, near_ref, moment_ref, own_ref):
    blocks = fields_ref.shape[0]
    centre = centre_ref[...]

    @pl.loop(0, blocks // 4)
    def _(group):
        for part in range(4):
            index = group * 4 + part
            at = pl.ds(pl.multiple_of(index * LANES, LANES), LANES)
            near, moment_ref[:, at] = second_near(
                fields_ref[index], centre, weight_ref[pl.ds(index, 1), :]
            )
            near_ref[at, :] = near.T
            pos, _, square = particle_rows(fields_ref[index], centre)
            four = jnp.concatenate([pos * -2.0, square], axis=0)
            own_ref[:, at] = own_rows(four, jnp.ones_like(square))


def remote_second_kernel(capacity, me_ref, *refs):
    pieces, (slots_hbm, tables_hbm, active_hbm) = refs[:4], refs[4:7]
    gathered, own_ref, fields_ref, centre_ref, moments_ref, gradient_ref, out_ref = refs[7:14]
    weights, near0, near1, moment0, moment1, slots_ref, tables_ref, active_ref = refs[14:22]
    semaphore, small = refs[22:]
    blocks = fields_ref.shape[0]
    partners = slots_ref.shape[0]
    copies = fetch(pieces, weights, semaphore)
    for number, (source, target) in enumerate(
        ((slots_hbm, slots_ref), (tables_hbm, tables_ref), (active_hbm, active_ref))
    ):
        copies += fetch((source,), target, small.at[pl.ds(number, 1)])
    for copy in copies:
        copy.wait()
    centre = centre_ref[...]
    me = me_ref[0]
    sides = ((near0, moment0), (near1, moment1))

    def take(pair, k):
        rows = [
            slot_rows(slots_ref[k, pair * 2 + odd], tables_ref, me, capacity) for odd in range(2)
        ]
        return [(gathered[row], weights[pl.ds(line, 1), :]) for row, line in rows]

    def build(fields, side, k):
        near, moment = sides[side]
        at = slice(k * LANES, (k + 1) * LANES)
        rows = []
        for odd in range(2):
            values, moments = second_near(fields[odd][0], centre, fields[odd][1])
            rows.append(values)
            moment[odd * 16 : odd * 16 + 16, at] = moments
        near[at, :] = jnp.concatenate(rows, axis=0).T

    def sums(pair, side, beside):
        near, moment = sides[side]
        at = pl.ds(pl.multiple_of(pair * 2 * LANES, 2 * LANES), 2 * LANES)
        _, total = pair_sums(diagonal(own_ref[:, at]), near, moment, None, 256, beside)
        before = moments_ref[0:4, at]
        for odd in range(2):
            index = pair * 2 + odd
            here = slice(odd * LANES, (odd + 1) * LANES)
            part = fold_rows(total[odd * 16 : odd * 16 + 16, here], 4) + before[:, here]
            pos, _, _ = particle_rows(fields_ref[index], centre)
            out = gradient_ref[:, index, :] + (pos * part[3:4] - part[0:3])
            out_ref[:, index, :] = jnp.where(active_ref[index] > 0, out, 0.0)

    in_turn(blocks // 2, partners, take, build, sums)


def join_kernel(parts, *refs):
    pieces, outs, semaphore = refs[: sum(parts)], refs[sum(parts) : -1], refs[-1]
    copies = []
    first = 0
    for out, count in zip(outs, parts):
        copies += fetch(pieces[first : first + count], out, semaphore.at[pl.ds(first, count)])
        first += count
    for copy in copies:
        copy.wait()


def in_vmem(count):
    return [pl.BlockSpec(memory_space=pltpu.VMEM)] * count


def in_smem(count):
    return [pl.BlockSpec(memory_space=pltpu.SMEM)] * count


def in_any(count):
    return [pl.BlockSpec(memory_space=pl.ANY)] * count


def shape(*dims, dtype=f32):
    return jax.ShapeDtypeStruct(dims, dtype)


def room(mebibytes):
    return pltpu.CompilerParams(vmem_limit_bytes=mebibytes * 2**20)


def join(*groups):
    flat = [item for group in groups for item in group]
    outs = [
        shape(sum(item.shape[0] for item in group), *group[0].shape[1:]) for group in groups
    ]
    return pl.pallas_call(
        functools.partial(join_kernel, [len(group) for group in groups]),
        out_shape=outs,
        in_specs=in_any(len(flat)),
        out_specs=in_any(len(outs)),
        scratch_shapes=[pltpu.SemaphoreType.DMA((len(flat),))],
        compiler_params=room(4),
    )(*flat)


def assemble(extra, stack, devices, capacity):
    blocks = stack.shape[1]
    return pl.pallas_call(
        functools.partial(assemble_kernel, devices, capacity),
        out_shape=[
            shape(blocks, 8, LANES),
            shape(blocks + extra, 8, LANES),
        ],
        in_specs=in_vmem(1),
        out_specs=in_vmem(2),
        compiler_params=room(8),
    )(stack)


def prepare(fields):
    particles = fields.shape[0] * LANES
    return pl.pallas_call(
        prepare_kernel,
        out_shape=[
            shape(particles, FEATS, dtype=bf16),
            shape(32, particles, dtype=bf16),
            shape(LANES, fields.shape[0]),
            shape(FEATS, particles, dtype=bf16),
            shape(8, LANES),
        ],
        in_specs=in_vmem(1),
        out_specs=in_vmem(5),
        compiler_params=room(16),
    )(fields)


def prepare_second(fields, centre, weight):
    particles = fields.shape[0] * LANES
    return pl.pallas_call(
        prepare_second_kernel,
        out_shape=[
            shape(particles, FEATS, dtype=bf16),
            shape(16, particles, dtype=bf16),
            shape(FEATS, particles, dtype=bf16),
        ],
        in_specs=in_vmem(3),
        out_specs=in_vmem(3),
        compiler_params=room(16),
    )(fields, centre, weight)


def local_pass(kernel, first, count, own, whole, sums):
    particles = own.shape[1]
    here = lambda index: (0, first + index)
    height = 16 if kernel is local_first_kernel else 8
    aliases = {}
    operands = [own, *whole]
    in_specs = [pl.BlockSpec((FEATS, TILE), here)]
    in_specs += in_vmem(len(whole))
    if sums is not None:
        aliases = {len(operands): 0}
        operands.append(sums)
        in_specs += in_any(1)
    return pl.pallas_call(
        kernel,
        grid=(count,),
        in_specs=in_specs,
        out_specs=pl.BlockSpec((height, TILE), here),
        out_shape=shape(height, particles),
        input_output_aliases=aliases,
        cost_estimate=pl.CostEstimate(
            flops=3 * TILE * particles * 2000, bytes_accessed=2**20, transcendentals=0
        ),
        compiler_params=room(24),
    )(*operands)


def swap(value, bit, devices):
    return lax.ppermute(value, "dom", [(i, i ^ bit) for i in range(devices)])


def places(order, devices):
    table = np.zeros((devices,), np.int32)
    for apart in range(devices):
        table[apart] = sum(1 << k for k, bit in enumerate(order) if apart & bit)
    return table


def combinations(group):
    return group if len(group) == 1 else [group[0], group[1], group[0] | group[1]]


def shares(tiles, weights):
    cuts = [
        round(tiles * sum(weights[:stage]) / sum(weights)) for stage in range(len(weights) + 1)
    ]
    return list(zip(cuts[:-1], cuts[1:]))


def per_device(
    devices,
    positions,
    velocities,
    masses,
    smoothing,
    entropy,
    export_blocks,
    partner_slots,
    active,
):
    blocks = positions.shape[0]
    particles = blocks * LANES
    capacity = export_blocks.shape[2]
    half = blocks // 2
    me = lax.axis_index("dom")
    extra = -(-devices * capacity // (8 * LANES))
    table = export_blocks.reshape(devices // blocks, blocks, capacity)
    layers = [
        jnp.transpose(positions, (1, 0, 2)),
        jnp.transpose(velocities, (1, 0, 2)),
        masses[None],
        smoothing[None],
    ]
    height = 8 + table.shape[0]
    stack = jnp.pad(table, ((8, 0), (0, 0), (0, LANES - capacity))).astype(f32)
    start = 0
    for layer in layers:
        after = height - start - layer.shape[0]
        stack = stack + jnp.pad(layer, ((start, after), (0, 0), (0, 0)))
        start += layer.shape[0]
    fields, payload = assemble(extra, stack, devices, capacity)
    bits = [1 << k for k in range(devices.bit_length() - 1)]
    groups = [bits[k : k + 2] for k in range(3, len(bits), 2)][::-1]
    split = groups[-1][-1]
    far = [bit for group in groups for bit in group]
    near_first = [bit for bit in far if bit != split] + [bits[2], bits[1], bits[0]]
    near_second = [bit for bit in far if bit != split] + [bits[1], bits[2], bits[0]]
    in_second = np.arange(devices) & split > 0
    payload_place = np.where(
        in_second, devices // 2 + places(near_second, devices), places(near_first, devices)
    )
    place = jnp.asarray(
        np.stack([payload_place, places(far + [bits[2], bits[1], bits[0]], devices)]), jnp.int32
    )
    tiles = particles // TILE
    stages = len(groups) + 3
    far_stages = [5] * len(groups)

    near, moment, root, own, centre = prepare(fields)
    sums = None
    first, second = [payload], []
    for number, (start, stop) in enumerate(shares(tiles, far_stages + [3, 6, 2])):
        if number < len(groups):
            group = groups[number]
            first += [swap(payload, bit, devices) for bit in combinations(group)]
        else:
            last = number - len(groups)
            first += [swap(item, [bits[2], bits[1], bits[0]][last], devices) for item in first]
            second += [swap(item, [bits[1], bits[2], bits[0]][last], devices) for item in second]
        if stop > start:
            sums = local_pass(
                local_first_kernel, start, stop - start, own, (near, moment, root), sums
            )
        if number < stages - 1:
            first, second, near, sums = lax.optimization_barrier((first, second, near, sums))
        if number < len(groups) - 1:
            (payload,) = join(first)
            first = [payload]
        elif number == len(groups) - 1:
            middle = len(first) // 2
            first, second = join(first[:middle], first[middle:])
            first, second = [first], [second]
        elif number < stages - 2:
            first, second = join(first, second)
            first, second = [first], [second]
    pieces = (*first, *second)

    me_array = me.astype(jnp.int32).reshape(1)

    rows = sum(piece.shape[0] for piece in pieces)
    slots = jnp.transpose(partner_slots)
    partners = slots.shape[0] * LANES
    near_side = [pltpu.VMEM((partners, 2 * FEATS), bf16)] * 2
    density, divergence, weight, gradient, tables, gathered = pl.pallas_call(
        functools.partial(remote_first_kernel, capacity, extra),
        out_shape=[
            shape(blocks, LANES),
            shape(blocks, LANES),
            shape(blocks, LANES),
            shape(3, blocks, LANES),
            shape(devices, LANES, dtype=jnp.int32),
            shape(rows, 8, LANES),
        ],
        in_specs=in_smem(1) + in_any(PIECES + 3) + in_vmem(4),
        out_specs=in_vmem(6),
        scratch_shapes=[
            pltpu.SMEM((devices, LANES), jnp.int32),
            *near_side,
            pltpu.VMEM((64, partners), bf16),
            pltpu.VMEM((64, partners), bf16),
            pltpu.VMEM((partners // LANES * 2, LANES), f32),
            pltpu.VMEM((partners // LANES * 2, LANES), f32),
            pltpu.VMEM((blocks, 16, LANES), f32),
            pltpu.SMEM(slots.shape, jnp.int32),
            pltpu.SMEM(place.shape, jnp.int32),
            pltpu.VMEM(entropy.shape, f32),
            pltpu.SemaphoreType.DMA((PIECES,)),
            pltpu.SemaphoreType.DMA,
            pltpu.SemaphoreType.DMA((3,)),
        ],
        compiler_params=room(20 + rows // 256),
    )(me_array, *pieces, slots, place, entropy, own, fields, centre, sums)

    near2, moment2, own2 = prepare_second(fields, centre, weight)
    sums = None
    weights = [weight]
    order = far + [bits[2], bits[1], bits[0]]
    for number, (start, stop) in enumerate(shares(tiles, [3] * (len(order) - 2) + [5, 2])):
        weights += [swap(item, order[number], devices) for item in weights]
        if stop > start:
            sums = local_pass(
                local_second_kernel, start, stop - start, own2, (near2, moment2), sums
            )
        if number < len(order) - 1:
            weights, near2, sums = lax.optimization_barrier((weights, near2, sums))
        if number < len(order) - 2:
            weights = list(join(weights))

    acceleration = pl.pallas_call(
        functools.partial(remote_second_kernel, capacity),
        out_shape=shape(3, blocks, LANES),
        in_specs=in_smem(1) + in_any(7) + in_vmem(6),
        out_specs=pl.BlockSpec(memory_space=pltpu.VMEM),
        scratch_shapes=[
            pltpu.VMEM((devices * blocks, LANES), f32),
            *near_side,
            pltpu.VMEM((32, partners), bf16),
            pltpu.VMEM((32, partners), bf16),
            pltpu.SMEM(slots.shape, jnp.int32),
            pltpu.SMEM(tables.shape, jnp.int32),
            pltpu.SMEM(active.shape, jnp.int32),
            pltpu.SemaphoreType.DMA((4,)),
            pltpu.SemaphoreType.DMA((3,)),
        ],
        compiler_params=room(20 + rows // 256),
    )(
        me_array, *weights, slots, tables, active, gathered, own2, fields, centre,
        sums, gradient,
    )
    return (density, divergence, jnp.transpose(acceleration, (1, 0, 2)))


def solution(mesh):
    in_specs = (
        P("dom", None, None),
        P("dom", None, None),
        P("dom", None),
        P("dom", None),
        P("dom", None),
        P("dom", None, None),
        P("dom", None),
        P("dom"),
    )
    out_specs = (P("dom", None), P("dom", None), P("dom", None, None))
    return jax.shard_map(
        functools.partial(per_device, mesh.shape["dom"]),
        mesh=mesh,
        in_specs=in_specs,
        out_specs=out_specs,
        check_vma=False,
    )
```
